128 devices in a mesh: gx: 8 (over y, core), gy: 16 (over z, x).
Axes of the slice: x: 4, y: 4, z: 4, core: 2. Of those that a mesh axis runs over, the one named last changes fastest.
Arguments:
- hidden: bfloat16 [1024, 16384], P('gx', 'gy'), as said below
- gain: bfloat16 [16384], P('gy'), may hold values from 0.099609375 to 1.8984375
- w_query: bfloat16 [16384, 16384], P('gy', 'gx'), may hold values from -0.046875 to 0.046875
- w_key: bfloat16 [16384, 1024], P('gy', 'gx'), may hold values from -0.125 to 0.125
- w_value: bfloat16 [16384, 1024], P('gy', 'gx'), may hold values from -0.046875 to 0.046875
- w_out: bfloat16 [16384, 16384], P('gx', 'gy'), may hold values from -0.046875 to 0.046875
- key_cache: bfloat16 [512, 1024, 1024], P('gy', None, 'gx'), as said below
- value_cache: bfloat16 [512, 1024, 1024], P('gy', None, 'gx'), may hold values from -6 to 6
- lengths: int32 [512], P('gy'), may hold values from 4 to 1024, as said below
Outputs:
- layer_out: bfloat16 [1024, 16384], P('gx', 'gy')
- new_keys: bfloat16 [1024, 1024], P('gy', 'gx')
- new_values: bfloat16 [1024, 1024], P('gy', 'gx')
The draws below stay inside these ranges and needn't reach their ends.
Inputs may be any that keep to these rules, and one draw needn't show every extreme that they name: `lengths`: each sequence's live cache slots; some sequence has all 1024 in every draw. `hidden`: residual stream entries. `key_cache`: cached keys.
All inputs are finite; a program needn't handle non-finite values.
Results may differ from the reference program's by a relative error of at most 0.0058.
Values may be sent and summed in bfloat16 or wider, within the bound.
No kernel may reach another device: no remote copies, remote signals or barrier semaphores. Data moves between devices by JAX's collectives and lax.ppermute only.
A program may use at most 128 MiB of HBM per device.

```python
import jax
import jax.numpy as jnp
from jax import lax

D = 16384
HQ = 128
KVH = 8
HD = 128
NEW = 2
SEQ_DEV = 32
SLOTS = 1024
NSEQ = 512
TOKENS = 1024


def draw_hidden(key, part):
    key = jax.random.fold_in(key, 11)
    subkeys = jax.random.split(key, 3)
    row_scale = jnp.exp(jax.random.uniform(subkeys[0], (TOKENS, 1), jnp.float32, 0.0, jnp.log(10.0)))
    col_scale = jnp.exp(jax.random.uniform(subkeys[1], (1, D), jnp.float32, jnp.log(0.3), jnp.log(3.0)))
    entries = jax.random.normal(subkeys[2], (TOKENS, D), jnp.float32)
    return (0.1 * entries * row_scale * col_scale).astype(jnp.bfloat16)


def draw_key_cache(key, part):
    key = jax.random.fold_in(key, 23)
    subkeys = jax.random.split(key, 1)
    width = KVH * HD
    entries = 1.5 * jax.random.normal(subkeys[0], (NSEQ, SLOTS, width), jnp.float32)
    return entries.astype(jnp.bfloat16)


def draw_lengths(key, part):
    key = jax.random.fold_in(key, 37)
    subkeys = jax.random.split(key, 3)
    blocks = NSEQ // SEQ_DEV
    ceilings = jax.random.randint(subkeys[0], (blocks, 1), max(4, SLOTS // 8), SLOTS + 1)
    drawn = jax.random.randint(subkeys[1], (blocks, SEQ_DEV), 4, ceilings + 1).reshape(-1)
    chosen = jax.random.randint(subkeys[2], (), 0, NSEQ)
    return jnp.where(jnp.arange(NSEQ, dtype=jnp.int32) == chosen, SLOTS, drawn).astype(jnp.int32)


def block_levels(key, shape, cuts, low, high):
    factor_of = 1.0
    for position, parts in cuts:
        draws = jax.random.uniform(jax.random.fold_in(jax.random.fold_in(key, 6), position), (parts,), jnp.float32, low / len(cuts), high / len(cuts))
        factor_of = factor_of * jnp.repeat(jnp.exp(draws), shape[position] // parts).reshape((-1,) + (1,) * (len(shape) - 1 - position))
    return factor_of


def normal_values(rng, shape, spread, limit, cuts=(), held_as=jnp.bfloat16):
    values = spread * jax.random.normal(rng, shape, jnp.float32)
    if cuts:
        values = values * block_levels(rng, shape, cuts, -0.22, 0.18)
    return jnp.clip(values, -limit, limit).astype(held_as)


def setup_inputs(seed: int = 0) -> dict:
    key_of = jax.random.split(jax.random.key(seed), 10)
    return {
        "hidden": draw_hidden(jax.random.fold_in(key_of[9], 71), 0),
        "gain": jnp.clip(1.0 + 0.18 * jax.random.normal(key_of[1], (D,), jnp.float32), 0.099609375, 1.8984375).astype(jnp.bfloat16),
        "w_query": normal_values(key_of[2], (D, HQ * HD), D ** -0.5, 0.046875, ((0, 16), (1, 8))),
        "w_key": normal_values(key_of[3], (D, KVH * HD), (D // 9) ** -0.5, 0.125, ((0, 16), (1, 8))),
        "w_value": normal_values(key_of[4], (D, KVH * HD), D ** -0.5, 0.046875, ((0, 16), (1, 8))),
        "w_out": normal_values(key_of[5], (HQ * HD, D), (HQ * HD) ** -0.5, 0.046875, ((0, 8), (1, 16))),
        "key_cache": draw_key_cache(jax.random.fold_in(key_of[9], 71), 0),
        "value_cache": normal_values(key_of[7], (NSEQ, SLOTS, KVH * HD), 1.0, 6.0, ((0, 16), (2, 8))),
        "lengths": draw_lengths(jax.random.fold_in(key_of[9], 71), 0),
    }


EPSILON = 1e-05
ROPE_BASE = 500000.0

def rotate(values, positions):
    half_dim = values.shape[-1] // 2
    indices = jnp.arange(half_dim, dtype=jnp.float32)
    inverse = jnp.power(jnp.float32(ROPE_BASE), -2.0 * indices / values.shape[-1])
    angles = positions.astype(jnp.float32)[:, None] * inverse[None, :]
    cosine = jnp.cos(angles)[:, None, :]
    sine = jnp.sin(angles)[:, None, :]
    first_half = values[..., :half_dim]
    second_half = values[..., half_dim:]
    return jnp.concatenate([first_half * cosine - second_half * sine, second_half * cosine + first_half * sine], -1)

def attend(queries, keys_new, values_new, cache_keys, cache_values, lengths):
    scale = HD ** (-0.5)
    query_f = queries.astype(jnp.float32)
    cache_scores = jnp.einsum('stgd,spd->stgp', query_f, cache_keys.astype(jnp.float32)) * scale
    fresh_scores = jnp.einsum('stgd,sud->stgu', query_f, keys_new.astype(jnp.float32)) * scale
    live = jnp.arange(cache_keys.shape[1], dtype=jnp.int32)[None, :] < lengths[:, None]
    cache_scores = jnp.where(live[:, None, None, :], cache_scores, -jnp.inf)
    causal = jnp.arange(NEW, dtype=jnp.int32)[None, :] <= jnp.arange(NEW, dtype=jnp.int32)[:, None]
    fresh_scores = jnp.where(causal[None, :, None, :], fresh_scores, -jnp.inf)
    highest = jnp.maximum(lax.optimization_barrier(jnp.max(cache_scores, -1)), lax.optimization_barrier(jnp.max(fresh_scores, -1)))[..., None]
    cache_exp = jnp.exp(cache_scores - highest)
    fresh_exp = jnp.exp(fresh_scores - highest)
    total = lax.optimization_barrier(jnp.sum(cache_exp, -1, keepdims=True)) + lax.optimization_barrier(jnp.sum(fresh_exp, -1, keepdims=True))
    cache_probs = (cache_exp / total).astype(jnp.bfloat16)
    fresh_probs = (fresh_exp / total).astype(jnp.bfloat16)
    context = jnp.einsum('stgp,spd->stgd', cache_probs.astype(jnp.float32), cache_values.astype(jnp.float32))
    context = context + jnp.einsum('stgu,sud->stgd', fresh_probs.astype(jnp.float32), values_new.astype(jnp.float32))
    return context.astype(jnp.bfloat16)

def reference(hidden, gain, w_query, w_key, w_value, w_out, key_cache, value_cache, lengths):
    inputs = hidden.astype(jnp.float32)
    inv_rms = lax.rsqrt(lax.optimization_barrier(jnp.mean(inputs * inputs, axis=1)) + EPSILON)[:, None]
    scaled_in = (inputs * gain.astype(jnp.float32)[None, :]).astype(jnp.bfloat16)
    query = inv_rms * jnp.dot(scaled_in, w_query, preferred_element_type=jnp.float32)
    key_raw = inv_rms * jnp.dot(scaled_in, w_key, preferred_element_type=jnp.float32)
    new_values = (inv_rms * jnp.dot(scaled_in, w_value, preferred_element_type=jnp.float32)).astype(jnp.bfloat16)
    token_count = hidden.shape[0]
    seq_count = lengths.shape[0]
    positions = (lengths[:, None] + jnp.arange(NEW, dtype=jnp.int32)[None, :]).reshape(-1)
    rotated_query = rotate(query.reshape(token_count, HQ, HD), positions).astype(jnp.bfloat16)
    new_keys = rotate(key_raw.reshape(token_count, KVH, HD), positions).astype(jnp.bfloat16)
    group = HQ // KVH
    query_grid = rotated_query.reshape(seq_count, NEW, KVH, group, HD)
    key_grid = new_keys.reshape(seq_count, NEW, KVH, HD)
    value_grid = new_values.reshape(seq_count, NEW, KVH, HD)
    cache_k = key_cache.reshape(seq_count, SLOTS, KVH, HD)
    cache_v = value_cache.reshape(seq_count, SLOTS, KVH, HD)
    results = []
    for kv_head in range(KVH):
        results.append(attend(query_grid[:, :, kv_head], key_grid[:, :, kv_head], value_grid[:, :, kv_head], cache_k[:, :, kv_head], cache_v[:, :, kv_head], lengths))
    context = jnp.stack(results, 2).reshape(token_count, HQ * HD)
    mixed = jnp.dot(context, w_out, preferred_element_type=jnp.float32)
    layer_out = (inputs + mixed).astype(jnp.bfloat16)
    return (layer_out, new_keys.reshape(token_count, KVH * HD), new_values)
```

```python
import functools

import jax
import jax.numpy as jnp
from jax import lax
from jax.experimental import pallas as pl
from jax.experimental.pallas import tpu as pltpu
from jax.sharding import PartitionSpec as P

D = 16384
HD = 128
NEW = 2
EPSILON = 1e-05
ROPE_BASE = 500000.0

NY = NZ = NX = 4
NC = 2
AXES = ("gx", "gy")
BF16 = jnp.bfloat16
F32 = jnp.float32
VMEM_LIMIT = 60 * 1024 * 1024


def pairs(move):
    out = []
    for y in range(NY):
        for c in range(NC):
            for z in range(NZ):
                for x in range(NX):
                    y2, c2, z2, x2 = move(y, c, z, x)
                    source = ((y * NC + c) * NZ + z) * NX + x
                    target = (((y2 % NY) * NC + c2 % NC) * NZ + z2 % NZ) * NX + x2 % NX
                    out.append((source, target))
    return out


def swap_core(value):
    return lax.ppermute(value, AXES, pairs(lambda y, c, z, x: (y, c + 1, z, x)))


def shift_y(value, step):
    return lax.ppermute(value, AXES, pairs(lambda y, c, z, x: (y + step, c, z, x)))


def shift_first(value, step):
    def move(y, c, z, x):
        return (y, c, z, x + step) if c == 0 else (y, c, z + step, x)

    return lax.ppermute(value, AXES, pairs(move))


def shift_second(value, step):
    def move(y, c, z, x):
        return (y, c, z + step, x) if c == 0 else (y, c, z, x + step)

    return lax.ppermute(value, AXES, pairs(move))


VSPEC = pl.BlockSpec(memory_space=pltpu.VMEM)
SSPEC = pl.BlockSpec(memory_space=pltpu.SMEM)
ANYSPEC = pl.BlockSpec(memory_space=pl.ANY)


def call(body, outs, in_specs, name, scratch=(), flops=0, moved=0):
    return pl.pallas_call(
        body,
        out_shape=outs,
        in_specs=in_specs,
        out_specs=[VSPEC] * len(outs),
        scratch_shapes=list(scratch),
        compiler_params=pltpu.CompilerParams(vmem_limit_bytes=VMEM_LIMIT),
        cost_estimate=pl.CostEstimate(flops=flops, bytes_accessed=moved, transcendentals=0),
        name=name,
    )


def shape(dims, dtype=BF16):
    return jax.ShapeDtypeStruct(dims, dtype)


def split_high_low(total):
    high = total.astype(BF16).astype(F32)
    return jnp.concatenate([high, total - high], axis=0).astype(BF16)


def scale_body(rows, pos_ref, gain_ref, *refs):
    blocks, (hs_ref, sq_ref) = refs[:8], refs[8:]
    gain = gain_ref[...].astype(F32)
    ones = jnp.ones((8, gain.shape[1]), BF16)
    pad = jnp.zeros((HD - rows, gain.shape[1]), BF16)
    for i, block in enumerate(blocks):
        for j in range(2):
            value = block[j * rows : (j + 1) * rows, :].astype(F32)
            slot = pos_ref[2 * i + j]
            hs_ref[slot] = (value * gain).astype(BF16)
            square = value * value
            high = square.astype(BF16)
            low = (square - high.astype(F32)).astype(BF16)
            total = jnp.zeros((8, HD), F32)
            for part in (high, low):
                total += lax.dot_general(
                    ones,
                    jnp.concatenate([part, pad], axis=0),
                    (((1,), (1,)), ((), ())),
                    preferred_element_type=F32,
                )
            sq_ref[slot] = split_high_low(total)


def project_body(rows, heads, group, hs_ref, sq_ref, wq_ref, wkv_ref, out_ref):
    depth = hs_ref.shape[2]
    lhs = hs_ref[4 * group : 4 * group + 4].reshape(4 * rows, depth)
    for n in range(heads // 2 + 1):
        rhs = wkv_ref[...] if n == heads // 2 else wq_ref[:, n * 256 : (n + 1) * 256]
        acc = jnp.dot(lhs, rhs, preferred_element_type=F32).astype(BF16)
        for f in range(4):
            for hh in range(2):
                head = 2 * n + hh
                out_ref[f, head * rows : (head + 1) * rows, :] = acc[
                    f * rows : (f + 1) * rows, hh * HD : (hh + 1) * HD
                ]
    for f in range(4):
        out_ref[f, (heads + 2) * rows :, :] = sq_ref[4 * group + f]


def first_sum_body(main, own_ref, r1_ref, r2_ref, r3_ref, *outs):
    for f in range(4):
        total = (
            own_ref[f].astype(F32)
            + r1_ref[f].astype(F32)
            + r2_ref[f].astype(F32)
            + r3_ref[f].astype(F32)
        )
        if f == 0:
            outs[0][...] = total
        else:
            outs[f][0:main, :] = total[:main].astype(BF16)
            outs[f][main:, :] = split_high_low(total[main : main + 8] + total[main + 8 :])


def attend_body(
    rows, heads, len_ref, p0_ref, r1_ref, r2_ref, r3_ref, cos_ref, sin_ref, kc_ref, vc_ref,
    ctx_ref, nk_ref, nv_ref, kbuf, vbuf, qs, os, kf, vf, sems,
):
    seqs = rows // NEW
    slots = kbuf.shape[1]
    main = (heads + 2) * rows

    def copies(s):
        return (
            pltpu.make_async_copy(kc_ref.at[s], kbuf.at[s], sems.at[s, 0]),
            pltpu.make_async_copy(vc_ref.at[s], vbuf.at[s], sems.at[s, 1]),
        )

    def start(s, carry):
        for copy in copies(s):
            copy.start()
        return carry

    lax.fori_loop(0, seqs, start, 0)

    def total(lo, hi):
        return (
            p0_ref[lo:hi, :]
            + r1_ref[lo:hi, :].astype(F32)
            + r2_ref[lo:hi, :].astype(F32)
            + r3_ref[lo:hi, :].astype(F32)
        )

    square = total(main, main + 16)
    column = jnp.transpose(square[:8] + square[8:])[:rows, 0:1]
    scales = lax.rsqrt(column / D + EPSILON)
    cosine, sine = cos_ref[...], sin_ref[...]

    def rope(value):
        return value * cosine + pltpu.roll(value, HD // 2, 1) * sine

    for head in range(heads):
        value = total(head * rows, (head + 1) * rows) * scales
        qs[pl.ds(head, rows, stride=heads), :] = rope(value).astype(BF16).astype(F32)
    key = rope(total(heads * rows, (heads + 1) * rows) * scales).astype(BF16)
    nk_ref[...] = key
    kf[...] = key.astype(F32)
    fresh = (total((heads + 1) * rows, (heads + 2) * rows) * scales).astype(BF16)
    nv_ref[...] = fresh
    vf[...] = fresh.astype(F32)

    per = NEW * heads
    scale = HD ** (-0.5)
    slot_of = lax.broadcasted_iota(jnp.int32, (per, slots), 1)
    second = lax.broadcasted_iota(jnp.int32, (per, 1), 0) >= heads

    def one(s):
        for copy in copies(s):
            copy.wait()
        query = qs[pl.ds(pl.multiple_of(s * per, per), per), :]
        k0, k1 = kf[pl.ds(2 * s, 1), :], kf[pl.ds(2 * s + 1, 1), :]
        v0, v1 = vf[pl.ds(2 * s, 1), :], vf[pl.ds(2 * s + 1, 1), :]
        s0 = jnp.sum(query * k0, axis=1, keepdims=True) * scale
        s1 = jnp.sum(query * k1, axis=1, keepdims=True) * scale
        s1 = jnp.where(second, s1, -jnp.inf)
        scores = (
            lax.dot_general(
                query.astype(BF16), kbuf[s], (((1,), (1,)), ((), ())), preferred_element_type=F32
            )
            * scale
        )
        scores = jnp.where(slot_of < len_ref[s], scores, -jnp.inf)
        highest = jnp.maximum(jnp.max(scores, axis=1, keepdims=True), jnp.maximum(s0, s1))
        probs = jnp.exp(scores - highest)
        p0, p1 = jnp.exp(s0 - highest), jnp.exp(s1 - highest)
        norm = 1.0 / (jnp.sum(probs, axis=1, keepdims=True) + p0 + p1)
        out = jnp.dot((probs * norm).astype(BF16), vbuf[s], preferred_element_type=F32)
        out += (p0 * norm).astype(BF16).astype(F32) * v0 + (p1 * norm).astype(BF16).astype(F32) * v1
        os[pl.ds(pl.multiple_of(s * per, per), per), :] = out

    def step(i, carry):
        for u in range(2):
            one(2 * i + u)
        return carry

    lax.fori_loop(0, seqs // 2, step, 0)
    for head in range(heads):
        ctx_ref[:, head * HD : (head + 1) * HD] = os[pl.ds(head, rows, stride=heads), :].astype(BF16)


def output_body(rows, pos_ref, *refs):
    a_refs, b_refs, (w_ref, mine_ref, theirs_ref) = refs[:4], refs[4:7], refs[7:]
    width = w_ref.shape[1]
    for f in range(4):
        if f == 0:
            lhs = jnp.concatenate([a[...] for a in a_refs], axis=0)
        else:
            lhs = b_refs[f - 1][...]
        for n in range(width // 256):
            cols = slice(n * 256, (n + 1) * 256)
            acc = jnp.dot(lhs, w_ref[:, cols], preferred_element_type=F32).astype(BF16)
            for e in range(4):
                slot = pos_ref[4 * f + e]
                part = acc[e * rows : (e + 1) * rows]

                @pl.when(slot < 8)
                def _(slot=slot, part=part, cols=cols):
                    mine_ref[slot, :, cols] = part

                @pl.when(slot >= 8)
                def _(slot=slot, part=part, cols=cols):
                    theirs_ref[slot - 8, :, cols] = part


def local(hidden, gain, w_query, w_key, w_value, w_out, key_cache, value_cache, lengths):
    seqs = key_cache.shape[0]
    slots = key_cache.shape[1]
    heads = w_query.shape[1] // HD
    rows = seqs * NEW
    depth = hidden.shape[1]
    width = w_out.shape[1]
    gx, gy = lax.axis_index("gx"), lax.axis_index("gy")
    y, c, z, x = gx // NC, gx % NC, gy // NX, gy % NX
    first_axis_x = c == 0

    positions = (lengths[:, None] + jnp.arange(NEW, dtype=jnp.int32)[None, :]).reshape(-1)
    indices = jnp.arange(HD // 2, dtype=F32)
    inverse = jnp.power(F32(ROPE_BASE), -2.0 * indices / HD)
    angles = positions.astype(F32)[:, None] * inverse[None, :]
    cosine, sine = jnp.cos(angles), jnp.sin(angles)
    cosine = jnp.concatenate([cosine, cosine], 1)
    sine = jnp.concatenate([-sine, sine], 1)
    w_kv = jnp.concatenate([w_key, w_value], 1)

    own = hidden
    received = [own] + [shift_y(own, d) for d in (1, 2, 3)]
    blocks = []
    for value in received:
        blocks += [value, swap_core(value)]

    places = []
    for d in range(4):
        for k in range(2):
            for j in range(2):
                zz, xx = (y - d) % 4, 2 * (c ^ k) + j
                dz, dx = (zz - z) % 4, (xx - x) % 4
                e, f = jnp.where(first_axis_x, dx, dz), jnp.where(first_axis_x, dz, dx)
                places.append(4 * e + f)
    places = jnp.stack(places).astype(jnp.int32)
    scaled, squares = call(
        functools.partial(scale_body, rows),
        [shape((16, rows, depth)), shape((16, 16, HD))],
        [SSPEC] + [VSPEC] * 9,
        "scale_rows",
        flops=4 * 16 * rows * depth,
        moved=8 * 16 * rows * depth,
    )(places, gain.reshape(1, -1), *blocks)

    main = (heads + 2) * rows
    length = main + 16

    def project(e):
        return call(
            functools.partial(project_body, rows, heads, e),
            [shape((4, length, HD))],
            [VSPEC] * 4,
            "project_%d" % e,
            flops=2 * 4 * rows * depth * (heads + 2) * HD,
            moved=2 * depth * (heads + 2) * HD,
        )(scaled, squares, w_query, w_kv)[0]

    sent = {e: shift_first(project(e), e) for e in (2, 1, 3)}
    kept = project(0)
    sums = call(
        functools.partial(first_sum_body, main),
        [shape((length, HD), F32)] + [shape((length, HD))] * 3,
        [VSPEC] * 4,
        "first_sum",
        flops=16 * length * HD,
        moved=10 * length * HD,
    )(kept, sent[1], sent[2], sent[3])
    arrived = [shift_second(sums[f], f) for f in (1, 2, 3)]

    context, fresh_keys, fresh_values = call(
        functools.partial(attend_body, rows, heads),
        [shape((rows, heads * HD)), shape((rows, HD)), shape((rows, HD))],
        [SSPEC] + [VSPEC] * 6 + [ANYSPEC] * 2,
        "attend",
        scratch=[
            pltpu.VMEM((seqs, slots, HD), BF16),
            pltpu.VMEM((seqs, slots, HD), BF16),
            pltpu.VMEM((rows * heads, HD), F32),
            pltpu.VMEM((rows * heads, HD), F32),
            pltpu.VMEM((rows, HD), F32),
            pltpu.VMEM((rows, HD), F32),
            pltpu.SemaphoreType.DMA((seqs, 2)),
        ],
        flops=4 * rows * heads * slots * HD,
        moved=4 * seqs * slots * HD,
    )(lengths, sums[0], *arrived, cosine, sine, key_cache, value_cache)

    near = [context] + [shift_first(context, e) for e in (1, 2, 3)]
    stacked = jnp.concatenate(near, axis=0)
    far = [shift_second(stacked, f) for f in (1, 2, 3)]
    places = []
    for f in range(4):
        for e in range(4):
            zz = jnp.where(first_axis_x, z - f, z - e) % 4
            xx = jnp.where(first_axis_x, x - e, x - f) % 4
            places.append(8 * ((xx // 2) ^ c) + 2 * ((zz - y) % 4) + xx % 2)
    places = jnp.stack(places).astype(jnp.int32)
    mine, theirs = call(
        functools.partial(output_body, rows),
        [shape((8, rows, width)), shape((8, rows, width))],
        [SSPEC] + [VSPEC] * 8,
        "project_out",
        flops=2 * 16 * rows * heads * HD * width,
        moved=2 * heads * HD * width,
    )(places, *near, *far, w_out)

    both = mine.astype(F32) + swap_core(theirs).astype(F32)
    both = both.reshape(4, 2 * rows, width)
    result = hidden.astype(F32) + both[0]
    for value in [shift_y(both[g].astype(BF16), g) for g in (1, 2, 3)]:
        result = result + value.astype(F32)
    return result.astype(BF16), fresh_keys, fresh_values


def solution(mesh):
    return jax.shard_map(
        local,
        mesh=mesh,
        in_specs=(
            P("gx", "gy"),
            P("gy"),
            P("gy", "gx"),
            P("gy", "gx"),
            P("gy", "gx"),
            P("gx", "gy"),
            P("gy", None, "gx"),
            P("gy", None, "gx"),
            P("gy"),
        ),
        out_specs=(P("gx", "gy"), P("gy", "gx"), P("gy", "gx")),
        check_vma=False,
    )
```

```python
import functools

import jax
import jax.numpy as jnp
from jax import lax
from jax.experimental import pallas as pl
from jax.experimental.pallas import tpu as pltpu
from jax.sharding import PartitionSpec as P

D = 16384
HD = 128
NEW = 2
EPSILON = 1e-05
ROPE_BASE = 500000.0

NY = NZ = NX = 4
NC = 2
AXES = ("gx", "gy")
BF16 = jnp.bfloat16
F32 = jnp.float32
MIB = 1024 * 1024
TOGETHER = 4


def pairs(move):
    out = []
    for y in range(NY):
        for c in range(NC):
            for z in range(NZ):
                for x in range(NX):
                    y2, c2, z2, x2 = move(y, c, z, x)
                    source = ((y * NC + c) * NZ + z) * NX + x
                    target = (((y2 % NY) * NC + c2 % NC) * NZ + z2 % NZ) * NX + x2 % NX
                    out.append((source, target))
    return out


def swap_core(value):
    return lax.ppermute(value, AXES, pairs(lambda y, c, z, x: (y, c + 1, z, x)))


def shift_y(value, step):
    return lax.ppermute(value, AXES, pairs(lambda y, c, z, x: (y + step, c, z, x)))


def shift_first(value, step):
    def move(y, c, z, x):
        return (y, c, z, x + step) if c == 0 else (y, c, z + step, x)

    return lax.ppermute(value, AXES, pairs(move))


def shift_second(value, step):
    def move(y, c, z, x):
        return (y, c, z + step, x) if c == 0 else (y, c, z, x + step)

    return lax.ppermute(value, AXES, pairs(move))


VSPEC = pl.BlockSpec(memory_space=pltpu.VMEM)
SSPEC = pl.BlockSpec(memory_space=pltpu.SMEM)
HSPEC = pl.BlockSpec(memory_space=pltpu.HBM)


def call(body, outs, in_specs, name, vmem, scratch=(), flops=0, moved=0):
    return pl.pallas_call(
        body,
        out_shape=outs,
        in_specs=in_specs,
        out_specs=[VSPEC] * len(outs),
        scratch_shapes=list(scratch),
        compiler_params=pltpu.CompilerParams(vmem_limit_bytes=vmem * MIB),
        cost_estimate=pl.CostEstimate(flops=flops, bytes_accessed=moved, transcendentals=0),
        name=name,
    )


def shape(dims, dtype=BF16):
    return jax.ShapeDtypeStruct(dims, dtype)


def in_hbm(value):
    return pltpu.with_memory_space_constraint(value, pltpu.HBM)


def place():
    gx, gy = lax.axis_index("gx"), lax.axis_index("gy")
    return gx // NC, gx % NC, gy // NX, gy % NX


def split_high_low(total):
    high = total.astype(BF16).astype(F32)
    return jnp.concatenate([high, total - high], axis=0).astype(BF16)


def load_body(back_ref, hidden_hbm, gain_hbm, wq_hbm, wk_hbm, wv_hbm, *refs):
    outs, sems = refs[:-1], refs[-1]
    sources = (back_ref, hidden_hbm, gain_hbm, wq_hbm, wk_hbm, wv_hbm)
    copies = [
        pltpu.make_async_copy(source, out, sems.at[i])
        for i, (source, out) in enumerate(zip(sources, outs))
    ]
    for copy in copies:
        copy.start()
    for copy in copies:
        copy.wait()


def project_group(rows, heads, group, hs, sq, wq_ref, wk_ref, wv_ref, outs):
    first, count = group[0], len(group)
    depth = hs.shape[2]
    lhs = hs[4 * first : 4 * (first + count)].reshape(4 * count * rows, depth)
    for n in range(heads // 2 + 1):
        if n == heads // 2:
            rhs = jnp.concatenate([wk_ref[...], wv_ref[...]], axis=1)
        else:
            rhs = wq_ref[:, n * 256 : (n + 1) * 256]
        acc = jnp.dot(lhs, rhs, preferred_element_type=F32).astype(BF16)
        for i in range(count):
            for f in range(4):
                top = (4 * i + f) * rows
                for hh in range(2):
                    head = 2 * n + hh
                    outs[i][f, head * rows : (head + 1) * rows, :] = acc[
                        top : top + rows, hh * HD : (hh + 1) * HD
                    ]
    for i in range(count):
        for f in range(4):
            outs[i][f, (heads + 2) * rows :, :] = sq[4 * (first + i) + f]


ORDER = (2, 1, 3, 0)


def project_first_body(rows, heads, gain_ref, wq_ref, wk_ref, wv_ref, *refs):
    blocks, (out_ref, hs, sq) = refs[:8], refs[8:]
    y, c, z, x = place()
    gain = gain_ref[...].astype(F32).reshape(1, -1)
    depth = gain.shape[1]
    ones = jnp.ones((8, depth), BF16)
    pad = jnp.zeros((HD - rows, depth), BF16)
    for i, block in enumerate(blocks):
        for j in range(2):
            value = block[j * rows : (j + 1) * rows, :].astype(F32)
            dz = (y - i // 2 - z) % 4
            dx = (2 * (c ^ (i % 2)) + j - x) % 4
            e, f = jnp.where(c == 0, dx, dz), jnp.where(c == 0, dz, dx)
            at = jnp.where(e == 2, 0, jnp.where(e == 0, 3, (e + 1) // 2))
            slot = 4 * at + f
            hs[slot] = (value * gain).astype(BF16)
            square = value * value
            high = square.astype(BF16)
            low = (square - high.astype(F32)).astype(BF16)
            total = jnp.zeros((8, HD), F32)
            for part in (high, low):
                total += lax.dot_general(
                    ones,
                    jnp.concatenate([part, pad], axis=0),
                    (((1,), (1,)), ((), ())),
                    preferred_element_type=F32,
                )
            sq[slot] = split_high_low(total)
    project_group(rows, heads, (0,), hs, sq, wq_ref, wk_ref, wv_ref, [out_ref])


def project_middle_body(rows, heads, token_ref, hs, sq, wq_ref, wk_ref, wv_ref, *outs):
    project_group(rows, heads, (1, 2), hs, sq, wq_ref, wk_ref, wv_ref, outs)


def project_last_body(
    rows, heads, hs, sq, wq_ref, wk_ref, wv_ref, kc_hbm, vc_hbm, out_ref, kc_ref, vc_ref, sems
):
    copies = [
        pltpu.make_async_copy(kc_hbm, kc_ref, sems.at[0]),
        pltpu.make_async_copy(vc_hbm, vc_ref, sems.at[1]),
    ]
    for copy in copies:
        copy.start()
    project_group(rows, heads, (3,), hs, sq, wq_ref, wk_ref, wv_ref, [out_ref])
    for copy in copies:
        copy.wait()


def first_sum_body(main, own_ref, r1_ref, r2_ref, r3_ref, *outs):
    for f in range(4):
        total = (
            own_ref[f].astype(F32)
            + r1_ref[f].astype(F32)
            + r2_ref[f].astype(F32)
            + r3_ref[f].astype(F32)
        )
        if f == 0:
            outs[0][...] = total
        else:
            outs[f][0:main, :] = total[:main].astype(BF16)
            outs[f][main:, :] = split_high_low(total[main : main + 8] + total[main + 8 :])


def attend_body(
    rows, heads, len_ref, p0_ref, r1_ref, r2_ref, r3_ref, cos_ref, sin_ref, kbuf, vbuf,
    ctx_ref, nk_ref, nv_ref, qs, os, kf, vf,
):
    seqs = rows // NEW
    slots = kbuf.shape[1]
    main = (heads + 2) * rows

    def total(lo, hi):
        return (
            p0_ref[lo:hi, :]
            + r1_ref[lo:hi, :].astype(F32)
            + r2_ref[lo:hi, :].astype(F32)
            + r3_ref[lo:hi, :].astype(F32)
        )

    square = total(main, main + 16)
    column = jnp.transpose(square[:8] + square[8:])[:rows, 0:1]
    scales = lax.rsqrt(column / D + EPSILON)
    cosine, sine = cos_ref[...], sin_ref[...]

    def rope(value):
        return value * cosine + pltpu.roll(value, HD // 2, 1) * sine

    for head in range(heads):
        value = total(head * rows, (head + 1) * rows) * scales
        qs[pl.ds(head, rows, stride=heads), :] = rope(value).astype(BF16).astype(F32)
    key = rope(total(heads * rows, (heads + 1) * rows) * scales).astype(BF16)
    nk_ref[...] = key
    kf[...] = key.astype(F32)
    fresh = (total((heads + 1) * rows, (heads + 2) * rows) * scales).astype(BF16)
    nv_ref[...] = fresh
    vf[...] = fresh.astype(F32)

    per = NEW * heads
    scale = HD ** (-0.5)
    slot_of = lax.broadcasted_iota(jnp.int32, (per, slots), 1)
    second = lax.broadcasted_iota(jnp.int32, (per, 1), 0) >= heads

    def several(first, count):
        ids = [first + u for u in range(count)]
        query = [qs[pl.ds(pl.multiple_of(s * per, per), per), :] for s in ids]
        scores = [
            lax.dot_general(
                q.astype(BF16), kbuf[s], (((1,), (1,)), ((), ())), preferred_element_type=F32
            )
            for q, s in zip(query, ids)
        ]
        scores = [
            jnp.where(slot_of < len_ref[s], v * scale, -jnp.inf) for v, s in zip(scores, ids)
        ]
        s0 = [
            jnp.sum(q * kf[pl.ds(2 * s, 1), :], axis=1, keepdims=True) * scale
            for q, s in zip(query, ids)
        ]
        s1 = [
            jnp.sum(q * kf[pl.ds(2 * s + 1, 1), :], axis=1, keepdims=True) * scale
            for q, s in zip(query, ids)
        ]
        s1 = [jnp.where(second, v, -jnp.inf) for v in s1]
        highest = [
            jnp.maximum(jnp.max(v, axis=1, keepdims=True), jnp.maximum(a, b))
            for v, a, b in zip(scores, s0, s1)
        ]
        probs = [jnp.exp(v - m) for v, m in zip(scores, highest)]
        p0 = [jnp.exp(v - m) for v, m in zip(s0, highest)]
        p1 = [jnp.exp(v - m) for v, m in zip(s1, highest)]
        norm = [
            1.0 / (jnp.sum(v, axis=1, keepdims=True) + a + b) for v, a, b in zip(probs, p0, p1)
        ]
        out = [
            jnp.dot((v * n).astype(BF16), vbuf[s], preferred_element_type=F32)
            for v, n, s in zip(probs, norm, ids)
        ]
        for u, s in enumerate(ids):
            w0 = (p0[u] * norm[u]).astype(BF16).astype(F32)
            w1 = (p1[u] * norm[u]).astype(BF16).astype(F32)
            os[pl.ds(pl.multiple_of(s * per, per), per), :] = (
                out[u] + w0 * vf[pl.ds(2 * s, 1), :] + w1 * vf[pl.ds(2 * s + 1, 1), :]
            )

    def step(i, carry):
        several(TOGETHER * i, TOGETHER)
        return carry

    lax.fori_loop(0, seqs // TOGETHER, step, 0)
    for head in range(heads):
        ctx_ref[:, head * HD : (head + 1) * HD] = os[pl.ds(head, rows, stride=heads), :].astype(BF16)


def output_body(count, *refs):
    a_refs, (w_ref, out_ref) = refs[:count], refs[count:]
    lhs = jnp.concatenate([a[...] for a in a_refs], axis=0) if count > 1 else a_refs[0][...]
    for n in range(w_ref.shape[1] // 256):
        cols = slice(n * 256, (n + 1) * 256)
        out_ref[:, cols] = jnp.dot(lhs, w_ref[:, cols], preferred_element_type=F32).astype(BF16)


def arrange_body(rows, *refs):
    y_refs, (mine_ref, theirs_ref) = refs[:4], refs[4:]
    y, c, z, x = place()
    for f in range(4):
        for e in range(4):
            zz = jnp.where(c == 0, z - f, z - e) % 4
            xx = jnp.where(c == 0, x - e, x - f) % 4
            slot = 2 * ((zz - y) % 4) + xx % 2
            part = y_refs[f][e * rows : (e + 1) * rows, :]
            own = xx // 2 == c

            @pl.when(own)
            def _(slot=slot, part=part):
                mine_ref[slot] = part

            @pl.when(jnp.logical_not(own))
            def _(slot=slot, part=part):
                theirs_ref[slot] = part


def local(hidden, gain, w_query, w_key, w_value, w_out, key_cache, value_cache, lengths):
    heads = w_query.shape[1] // HD
    depth = hidden.shape[1]
    width = w_out.shape[1]
    rows = key_cache.shape[0] * NEW
    main = (heads + 2) * rows
    length = main + 16

    positions = (lengths[:, None] + jnp.arange(NEW, dtype=jnp.int32)[None, :]).reshape(-1)
    indices = jnp.arange(HD // 2, dtype=F32)
    inverse = jnp.power(F32(ROPE_BASE), -2.0 * indices / HD)
    angles = positions.astype(F32)[:, None] * inverse[None, :]
    cosine, sine = jnp.cos(angles), jnp.sin(angles)
    cosine = jnp.concatenate([cosine, cosine], 1)
    sine = jnp.concatenate([-sine, sine], 1)

    received = [shift_y(hidden, d) for d in (1, 2, 3)]
    sources = [hidden, gain, w_query, w_key, w_value]
    back, own, scale, *weights = call(
        load_body,
        [pltpu.VMEM(v.shape, v.dtype) for v in [received[0]] + sources],
        [VSPEC] + [HSPEC] * 5,
        "load",
        4,
        scratch=[pltpu.SemaphoreType.DMA((6,))],
    )(received[0], *[in_hbm(v) for v in sources])
    blocks = [own, swap_core(hidden)]
    for value in [back] + received[1:]:
        blocks += [value, swap_core(value)]

    group = shape((4, length, HD))
    sent = {}
    kept = {}
    kept[2], scaled, squares = call(
        functools.partial(project_first_body, rows, heads),
        [group, shape((16, rows, depth)), shape((16, 16, HD))],
        [VSPEC] * 12,
        "project_first",
        12,
    )(scale, *weights, *blocks)
    sent[2] = shift_first(kept[2], 2)
    token = swap_core(squares[0])
    kept[1], kept[3] = call(
        functools.partial(project_middle_body, rows, heads),
        [group, group],
        [VSPEC] * 6,
        "project_middle",
        12,
    )(token, scaled, squares, *weights)
    sent[1], sent[3] = shift_first(kept[1], 1), shift_first(kept[3], 3)
    kept[0], keys, values = call(
        functools.partial(project_last_body, rows, heads),
        [group] + [pltpu.VMEM(v.shape, v.dtype) for v in (key_cache, value_cache)],
        [VSPEC] * 5 + [HSPEC] * 2,
        "project_last",
        12,
        scratch=[pltpu.SemaphoreType.DMA((2,))],
    )(scaled, squares, *weights, in_hbm(key_cache), in_hbm(value_cache))
    sums = call(
        functools.partial(first_sum_body, main),
        [shape((length, HD), F32)] + [shape((length, HD))] * 3,
        [VSPEC] * 4,
        "first_sum",
        10,
    )(kept[0], sent[1], sent[2], sent[3])
    parts = [sums[0]] + [shift_second(sums[f], f) for f in (1, 2, 3)]

    context, fresh_keys, fresh_values = call(
        functools.partial(attend_body, rows, heads),
        [shape((rows, heads * HD)), shape((rows, HD)), shape((rows, HD))],
        [SSPEC] + [VSPEC] * 8,
        "attend",
        10,
        scratch=[
            pltpu.VMEM((rows * heads, HD), F32),
            pltpu.VMEM((rows * heads, HD), F32),
            pltpu.VMEM((rows, HD), F32),
            pltpu.VMEM((rows, HD), F32),
        ],
    )(lengths, *parts, cosine, sine, keys, values)

    near = [context] + [shift_first(context, e) for e in (1, 2, 3)]
    stacked = jnp.concatenate(near, axis=0)
    far = [shift_second(stacked, f) for f in (1, 2, 3)]
    partial = []
    for rows_in in [stacked] + far:
        partial += call(
            functools.partial(output_body, 1),
            [shape((4 * rows, width))],
            [VSPEC] * 2,
            "project_out",
            8,
        )(rows_in, w_out)
    mine, theirs = call(
        functools.partial(arrange_body, rows),
        [shape((8, rows, width)), shape((8, rows, width))],
        [VSPEC] * 4,
        "arrange",
        8,
    )(*partial)
    both = mine.astype(F32) + swap_core(theirs).astype(F32)
    both = both.reshape(4, 2 * rows, width)
    result = hidden.astype(F32) + both[0]
    for value in [shift_y(both[g].astype(BF16), g) for g in (1, 2, 3)]:
        result = result + value.astype(F32)
    return result.astype(BF16), fresh_keys, fresh_values


def solution(mesh):
    return jax.shard_map(
        local,
        mesh=mesh,
        in_specs=(
            P("gx", "gy"),
            P("gy"),
            P("gy", "gx"),
            P("gy", "gx"),
            P("gy", "gx"),
            P("gx", "gy"),
            P("gy", None, "gx"),
            P("gy", None, "gx"),
            P("gy"),
        ),
        out_specs=(P("gx", "gy"), P("gy", "gx"), P("gy", "gx")),
        check_vma=False,
    )
```

```python
import functools

import jax
import jax.numpy as jnp
from jax import lax
from jax.experimental import pallas as pl
from jax.experimental.pallas import tpu as pltpu
from jax.sharding import PartitionSpec as P

D = 16384
HD = 128
NEW = 2
EPSILON = 1e-05
ROPE_BASE = 500000.0

NY = NZ = NX = 4
NC = 2
AXES = ("gx", "gy")
BF16 = jnp.bfloat16
F32 = jnp.float32
MIB = 1024 * 1024
TOGETHER = 4


def pairs(move):
    out = []
    for y in range(NY):
        for c in range(NC):
            for z in range(NZ):
                for x in range(NX):
                    y2, c2, z2, x2 = move(y, c, z, x)
                    source = ((y * NC + c) * NZ + z) * NX + x
                    target = (((y2 % NY) * NC + c2 % NC) * NZ + z2 % NZ) * NX + x2 % NX
                    out.append((source, target))
    return out


def swap_core(value):
    return lax.ppermute(value, AXES, pairs(lambda y, c, z, x: (y, c + 1, z, x)))


def shift_y(value, step):
    return lax.ppermute(value, AXES, pairs(lambda y, c, z, x: (y + step, c, z, x)))


def shift_first(value, step):
    def move(y, c, z, x):
        return (y, c, z, x + step) if c == 0 else (y, c, z + step, x)

    return lax.ppermute(value, AXES, pairs(move))


def shift_second(value, step):
    def move(y, c, z, x):
        return (y, c, z + step, x) if c == 0 else (y, c, z, x + step)

    return lax.ppermute(value, AXES, pairs(move))


VSPEC = pl.BlockSpec(memory_space=pltpu.VMEM)
SSPEC = pl.BlockSpec(memory_space=pltpu.SMEM)
HSPEC = pl.BlockSpec(memory_space=pltpu.HBM)


def call(body, outs, in_specs, name, vmem, scratch=(), flops=0, moved=0):
    return pl.pallas_call(
        body,
        out_shape=outs,
        in_specs=in_specs,
        out_specs=[VSPEC] * len(outs),
        scratch_shapes=list(scratch),
        compiler_params=pltpu.CompilerParams(vmem_limit_bytes=vmem * MIB),
        cost_estimate=pl.CostEstimate(flops=flops, bytes_accessed=moved, transcendentals=0),
        name=name,
    )


def shape(dims, dtype=BF16):
    return jax.ShapeDtypeStruct(dims, dtype)


def in_hbm(value):
    return pltpu.with_memory_space_constraint(value, pltpu.HBM)


def place():
    gx, gy = lax.axis_index("gx"), lax.axis_index("gy")
    return gx // NC, gx % NC, gy // NX, gy % NX


def split_high_low(total):
    high = total.astype(BF16).astype(F32)
    return jnp.concatenate([high, total - high], axis=0).astype(BF16)


def load_body(back_ref, hidden_hbm, gain_hbm, wq_hbm, wk_hbm, wv_hbm, *refs):
    outs, sems = refs[:-1], refs[-1]
    sources = (back_ref, hidden_hbm, gain_hbm, wq_hbm, wk_hbm, wv_hbm)
    copies = [
        pltpu.make_async_copy(source, out, sems.at[i])
        for i, (source, out) in enumerate(zip(sources, outs))
    ]
    for copy in copies:
        copy.start()
    for copy in copies:
        copy.wait()


def project_group(rows, heads, group, hs, sq, wq_ref, wk_ref, wv_ref, outs):
    first, count = group[0], len(group)
    depth = hs.shape[2]
    lhs = hs[4 * first : 4 * (first + count)].reshape(4 * count * rows, depth)
    per = outs[0].shape[0]
    for n in range(heads // 2 + 1):
        if n == heads // 2:
            rhs = jnp.concatenate([wk_ref[...], wv_ref[...]], axis=1)
        else:
            rhs = wq_ref[:, n * 256 : (n + 1) * 256]
        acc = jnp.dot(lhs, rhs, preferred_element_type=F32).astype(BF16)
        for i in range(4 * count):
            for hh in range(2):
                head = 2 * n + hh
                outs[i // per][i % per, head * rows : (head + 1) * rows, :] = acc[
                    i * rows : (i + 1) * rows, hh * HD : (hh + 1) * HD
                ]
    for i in range(4 * count):
        outs[i // per][i % per, (heads + 2) * rows :, :] = sq[4 * first + i]


def project_first_body(rows, heads, gain_ref, wq_ref, wk_ref, wv_ref, *refs):
    blocks, outs, (hs, sq) = refs[:8], refs[8:10], refs[10:]
    y, c, z, x = place()
    gain = gain_ref[...].astype(F32).reshape(1, -1)
    depth = gain.shape[1]
    ones = jnp.ones((8, depth), BF16)
    pad = jnp.zeros((HD - rows, depth), BF16)
    for i, block in enumerate(blocks):
        for j in range(2):
            value = block[j * rows : (j + 1) * rows, :].astype(F32)
            dz = (y - i // 2 - z) % 4
            dx = (2 * (c ^ (i % 2)) + j - x) % 4
            e, f = jnp.where(c == 0, dx, dz), jnp.where(c == 0, dz, dx)
            at = jnp.where(e == 2, 0, jnp.where(e == 0, 3, (e + 1) // 2))
            slot = 4 * at + f
            hs[slot] = (value * gain).astype(BF16)
            square = value * value
            high = square.astype(BF16)
            low = (square - high.astype(F32)).astype(BF16)
            total = jnp.zeros((8, HD), F32)
            for part in (high, low):
                total += lax.dot_general(
                    ones,
                    jnp.concatenate([part, pad], axis=0),
                    (((1,), (1,)), ((), ())),
                    preferred_element_type=F32,
                )
            sq[slot] = split_high_low(total)
    project_group(rows, heads, (0,), hs, sq, wq_ref, wk_ref, wv_ref, outs)


def project_middle_body(rows, heads, token_ref, hs, sq, wq_ref, wk_ref, wv_ref, *outs):
    project_group(rows, heads, (1, 2), hs, sq, wq_ref, wk_ref, wv_ref, outs)


def project_last_body(
    rows, heads, hs, sq, wq_ref, wk_ref, wv_ref, kc_hbm, vc_hbm, out_ref, kc_ref, vc_ref, sems
):
    copies = [
        pltpu.make_async_copy(kc_hbm, kc_ref, sems.at[0]),
        pltpu.make_async_copy(vc_hbm, vc_ref, sems.at[1]),
    ]
    for copy in copies:
        copy.start()
    project_group(rows, heads, (3,), hs, sq, wq_ref, wk_ref, wv_ref, [out_ref])
    for copy in copies:
        copy.wait()


def add_body(main, terms, *refs):
    ins, outs = refs[: len(refs) - len(terms)], refs[len(refs) - len(terms) :]
    for out, picks in zip(outs, terms):
        for i, pick in enumerate(picks):
            total = sum(ins[ref][block].astype(F32) for ref, block in pick)
            out[i, 0:main, :] = total[:main].astype(BF16)
            out[i, main:, :] = split_high_low(total[main : main + 8] + total[main + 8 :])


def attend_body(
    rows, heads, len_ref, p0_ref, p1_ref, p2_ref, r1_ref, r2_ref, r3_ref,
    cos_ref, sin_ref, kbuf, vbuf,
    ctx_ref, nk_ref, nv_ref, qs, os, kf, vf,
):
    seqs = rows // NEW
    slots = kbuf.shape[1]
    main = (heads + 2) * rows

    def total(lo, hi):
        refs = (p0_ref, p1_ref, p2_ref, r1_ref, r2_ref, r3_ref)
        return sum(ref[0, lo:hi, :].astype(F32) for ref in refs)

    square = total(main, main + 16)
    column = jnp.transpose(square[:8] + square[8:])[:rows, 0:1]
    scales = lax.rsqrt(column / D + EPSILON)
    cosine, sine = cos_ref[...], sin_ref[...]

    def rope(value):
        return value * cosine + pltpu.roll(value, HD // 2, 1) * sine

    for head in range(heads):
        value = total(head * rows, (head + 1) * rows) * scales
        qs[pl.ds(head, rows, stride=heads), :] = rope(value).astype(BF16).astype(F32)
    key = rope(total(heads * rows, (heads + 1) * rows) * scales).astype(BF16)
    nk_ref[...] = key
    kf[...] = key.astype(F32)
    fresh = (total((heads + 1) * rows, (heads + 2) * rows) * scales).astype(BF16)
    nv_ref[...] = fresh
    vf[...] = fresh.astype(F32)

    per = NEW * heads
    scale = HD ** (-0.5)
    slot_of = lax.broadcasted_iota(jnp.int32, (per, slots), 1)
    second = lax.broadcasted_iota(jnp.int32, (per, 1), 0) >= heads

    def several(first, count):
        ids = [first + u for u in range(count)]
        query = [qs[pl.ds(pl.multiple_of(s * per, per), per), :] for s in ids]
        scores = [
            lax.dot_general(
                q.astype(BF16), kbuf[s], (((1,), (1,)), ((), ())), preferred_element_type=F32
            )
            for q, s in zip(query, ids)
        ]
        scores = [
            jnp.where(slot_of < len_ref[s], v * scale, -jnp.inf) for v, s in zip(scores, ids)
        ]
        s0 = [
            jnp.sum(q * kf[pl.ds(2 * s, 1), :], axis=1, keepdims=True) * scale
            for q, s in zip(query, ids)
        ]
        s1 = [
            jnp.sum(q * kf[pl.ds(2 * s + 1, 1), :], axis=1, keepdims=True) * scale
            for q, s in zip(query, ids)
        ]
        s1 = [jnp.where(second, v, -jnp.inf) for v in s1]
        highest = [
            jnp.maximum(jnp.max(v, axis=1, keepdims=True), jnp.maximum(a, b))
            for v, a, b in zip(scores, s0, s1)
        ]
        probs = [jnp.exp(v - m) for v, m in zip(scores, highest)]
        p0 = [jnp.exp(v - m) for v, m in zip(s0, highest)]
        p1 = [jnp.exp(v - m) for v, m in zip(s1, highest)]
        norm = [
            1.0 / (jnp.sum(v, axis=1, keepdims=True) + a + b) for v, a, b in zip(probs, p0, p1)
        ]
        out = [
            jnp.dot((v * n).astype(BF16), vbuf[s], preferred_element_type=F32)
            for v, n, s in zip(probs, norm, ids)
        ]
        for u, s in enumerate(ids):
            w0 = (p0[u] * norm[u]).astype(BF16).astype(F32)
            w1 = (p1[u] * norm[u]).astype(BF16).astype(F32)
            os[pl.ds(pl.multiple_of(s * per, per), per), :] = (
                out[u] + w0 * vf[pl.ds(2 * s, 1), :] + w1 * vf[pl.ds(2 * s + 1, 1), :]
            )

    def step(i, carry):
        several(TOGETHER * i, TOGETHER)
        return carry

    lax.fori_loop(0, seqs // TOGETHER, step, 0)
    for head in range(heads):
        ctx_ref[:, head * HD : (head + 1) * HD] = os[pl.ds(head, rows, stride=heads), :].astype(BF16)


def output_body(a_ref, b_ref, w_ref, out_ref):
    lhs = jnp.concatenate([a_ref[...], b_ref[...]], axis=0)
    for n in range(w_ref.shape[1] // 256):
        cols = slice(n * 256, (n + 1) * 256)
        out_ref[:, cols] = jnp.dot(lhs, w_ref[:, cols], preferred_element_type=F32).astype(BF16)


def output_last_body(rows, a_ref, b_ref, w_ref, y0_ref, y1_ref, y3_ref, mine_ref, theirs_ref, y2):
    y, c, z, x = place()
    output_body(a_ref, b_ref, w_ref, y2)
    for f, source in enumerate((y0_ref, y1_ref, y2, y3_ref)):
        for e in range(4):
            zz = jnp.where(c == 0, z - f, z - e) % 4
            xx = jnp.where(c == 0, x - e, x - f) % 4
            slot = 2 * ((zz - y) % 4) + xx % 2
            top = e * rows
            own = xx // 2 == c

            @pl.when(own)
            def _(slot=slot, source=source, top=top):
                mine_ref[slot] = source[top : top + rows, :]

            @pl.when(jnp.logical_not(own))
            def _(slot=slot, source=source, top=top):
                theirs_ref[slot] = source[top : top + rows, :]


def local(hidden, gain, w_query, w_key, w_value, w_out, key_cache, value_cache, lengths):
    heads = w_query.shape[1] // HD
    depth = hidden.shape[1]
    width = w_out.shape[1]
    rows = key_cache.shape[0] * NEW
    main = (heads + 2) * rows
    length = main + 16

    positions = (lengths[:, None] + jnp.arange(NEW, dtype=jnp.int32)[None, :]).reshape(-1)
    indices = jnp.arange(HD // 2, dtype=F32)
    inverse = jnp.power(F32(ROPE_BASE), -2.0 * indices / HD)
    angles = positions.astype(F32)[:, None] * inverse[None, :]
    cosine, sine = jnp.cos(angles), jnp.sin(angles)
    cosine = jnp.concatenate([cosine, cosine], 1)
    sine = jnp.concatenate([-sine, sine], 1)

    received = [shift_y(hidden, d) for d in (1, 2, 3)]
    sources = [hidden, gain, w_query, w_key, w_value]
    back, own, scale, *weights = call(
        load_body,
        [pltpu.VMEM(v.shape, v.dtype) for v in [received[0]] + sources],
        [VSPEC] + [HSPEC] * 5,
        "load",
        4,
        scratch=[pltpu.SemaphoreType.DMA((6,))],
    )(received[0], *[in_hbm(v) for v in sources])
    blocks = [own, swap_core(hidden)]
    for value in [back] + received[1:]:
        blocks += [value, swap_core(value)]

    half = shape((2, length, HD))
    two_a, two_b, scaled, squares = call(
        functools.partial(project_first_body, rows, heads),
        [half, half, shape((16, rows, depth)), shape((16, 16, HD))],
        [VSPEC] * 12,
        "project_first",
        12,
    )(scale, *weights, *blocks)
    over_a, over_b = shift_first(two_a, 1), shift_first(two_b, 3)
    token = swap_core(squares[0])
    one_a, one_b, three_a, three_b = call(
        functools.partial(project_middle_body, rows, heads),
        [half] * 4,
        [VSPEC] * 6,
        "project_middle",
        12,
    )(token, scaled, squares, *weights)
    from_one_b, from_three_a = shift_first(one_b, 1), shift_first(three_a, 3)

    def add(terms, *values):
        return call(
            functools.partial(add_body, main, terms),
            [shape((len(picks), length, HD)) for picks in terms],
            [VSPEC] * len(values),
            "add",
            8,
        )(*values)

    pairwise = [[[(0, 0), (1, 0)], [(0, 1), (1, 1)]]]
    from_one_a = shift_first(add(pairwise, one_a, over_a)[0], 1)
    from_three_b = shift_first(add(pairwise, three_b, over_b)[0], 3)
    own_group, keys, values = call(
        functools.partial(project_last_body, rows, heads),
        [shape((4, length, HD))] + [pltpu.VMEM(v.shape, v.dtype) for v in (key_cache, value_cache)],
        [VSPEC] * 5 + [HSPEC] * 2,
        "project_last",
        12,
        scratch=[pltpu.SemaphoreType.DMA((2,))],
    )(scaled, squares, *weights, in_hbm(key_cache), in_hbm(value_cache))
    terms = [
        [[(0, 2), (3, 0), (4, 0)]],
        [[(0, 1), (1, 1), (2, 1)]],
        [[(0, 3), (3, 1), (4, 1)]],
    ]
    two, one, three = add(
        terms, own_group, from_one_a, from_three_a, from_one_b, from_three_b
    )
    arrived = [shift_second(two, 2), shift_second(one, 1), shift_second(three, 3)]
    parts = [own_group, from_one_a, from_three_a] + arrived

    context, fresh_keys, fresh_values = call(
        functools.partial(attend_body, rows, heads),
        [shape((rows, heads * HD)), shape((rows, HD)), shape((rows, HD))],
        [SSPEC] + [VSPEC] * 10,
        "attend",
        10,
        scratch=[
            pltpu.VMEM((rows * heads, HD), F32),
            pltpu.VMEM((rows * heads, HD), F32),
            pltpu.VMEM((rows, HD), F32),
            pltpu.VMEM((rows, HD), F32),
        ],
    )(lengths, *parts, cosine, sine, keys, values)

    one, three, two = shift_first(context, 1), shift_first(context, 3), shift_first(context, 2)
    low, high = jnp.concatenate([context, one], 0), jnp.concatenate([two, three], 0)
    one_low, three_high = shift_second(low, 1), shift_second(high, 3)
    two_low, two_high = shift_second(one_low, 1), shift_second(three_high, 3)
    one_high, three_low = shift_second(high, 1), shift_second(low, 3)

    def project_out(a, b):
        return call(
            output_body,
            [shape((4 * rows, width))],
            [VSPEC] * 3,
            "project_out",
            8,
        )(a, b, w_out)[0]

    mine, theirs = call(
        functools.partial(output_last_body, rows),
        [shape((8, rows, width)), shape((8, rows, width))],
        [VSPEC] * 6,
        "project_out_last",
        12,
        scratch=[pltpu.VMEM((4 * rows, width), BF16)],
    )(
        two_low,
        two_high,
        w_out,
        project_out(low, high),
        project_out(one_low, one_high),
        project_out(three_low, three_high),
    )
    both = mine.astype(F32) + swap_core(theirs).astype(F32)
    both = both.reshape(4, 2 * rows, width)
    result = hidden.astype(F32) + both[0]
    for value in [shift_y(both[g].astype(BF16), g) for g in (1, 2, 3)]:
        result = result + value.astype(F32)
    return result.astype(BF16), fresh_keys, fresh_values


def solution(mesh):
    return jax.shard_map(
        local,
        mesh=mesh,
        in_specs=(
            P("gx", "gy"),
            P("gy"),
            P("gy", "gx"),
            P("gy", "gx"),
            P("gy", "gx"),
            P("gx", "gy"),
            P("gy", None, "gx"),
            P("gy", None, "gx"),
            P("gy"),
        ),
        out_specs=(P("gx", "gy"), P("gy", "gx"), P("gy", "gx")),
        check_vma=False,
    )
```

```python
import functools

import jax
import jax.numpy as jnp
from jax import lax
from jax.experimental import pallas as pl
from jax.experimental.pallas import tpu as pltpu
from jax.sharding import PartitionSpec as P

D = 16384
HD = 128
NEW = 2
EPSILON = 1e-05
ROPE_BASE = 500000.0

NY = NZ = NX = 4
NC = 2
AXES = ("gx", "gy")
BF16 = jnp.bfloat16
F32 = jnp.float32
MIB = 1024 * 1024
TOGETHER = 8
LOG2_E = 1.4426950408889634


def pairs(move):
    out = []
    for y in range(NY):
        for c in range(NC):
            for z in range(NZ):
                for x in range(NX):
                    y2, c2, z2, x2 = move(y, c, z, x)
                    source = ((y * NC + c) * NZ + z) * NX + x
                    target = (((y2 % NY) * NC + c2 % NC) * NZ + z2 % NZ) * NX + x2 % NX
                    out.append((source, target))
    return out


def swap_core(value):
    return lax.ppermute(value, AXES, pairs(lambda y, c, z, x: (y, c + 1, z, x)))


def shift_y(value, step):
    return lax.ppermute(value, AXES, pairs(lambda y, c, z, x: (y + step, c, z, x)))


def shift_first(value, step):
    def move(y, c, z, x):
        return (y, c, z, x + step) if c == 0 else (y, c, z + step, x)

    return lax.ppermute(value, AXES, pairs(move))


def shift_second(value, step):
    def move(y, c, z, x):
        return (y, c, z + step, x) if c == 0 else (y, c, z, x + step)

    return lax.ppermute(value, AXES, pairs(move))


VSPEC = pl.BlockSpec(memory_space=pltpu.VMEM)
SSPEC = pl.BlockSpec(memory_space=pltpu.SMEM)
HSPEC = pl.BlockSpec(memory_space=pltpu.HBM)


def call(body, outs, in_specs, name, vmem, scratch=(), flops=0, moved=0):
    return pl.pallas_call(
        body,
        out_shape=outs,
        in_specs=in_specs,
        out_specs=[VSPEC] * len(outs),
        scratch_shapes=list(scratch),
        compiler_params=pltpu.CompilerParams(vmem_limit_bytes=vmem * MIB),
        cost_estimate=pl.CostEstimate(flops=flops, bytes_accessed=moved, transcendentals=0),
        name=name,
    )


def shape(dims, dtype=BF16):
    return jax.ShapeDtypeStruct(dims, dtype)


def in_hbm(value):
    return pltpu.with_memory_space_constraint(value, pltpu.HBM)


def place():
    gx, gy = lax.axis_index("gx"), lax.axis_index("gy")
    return gx // NC, gx % NC, gy // NX, gy % NX


def split_high_low(total):
    high = total.astype(BF16).astype(F32)
    return jnp.concatenate([high, total - high], axis=0).astype(BF16)


def load_body(back_ref, hidden_hbm, gain_hbm, wq_hbm, wk_hbm, wv_hbm, *refs):
    outs, sems = refs[:-1], refs[-1]
    sources = (back_ref, hidden_hbm, gain_hbm, wq_hbm, wk_hbm, wv_hbm)
    copies = [
        pltpu.make_async_copy(source, out, sems.at[i])
        for i, (source, out) in enumerate(zip(sources, outs))
    ]
    for copy in copies:
        copy.start()
    for copy in copies:
        copy.wait()


def project_blocks(rows, heads, first, hs, sq, wq_ref, wk_ref, wv_ref, outs):
    per = outs[0].shape[0]
    count = per * len(outs)
    lhs = hs[first : first + count].reshape(count * rows, hs.shape[2])
    for n in range(heads // 2 + 1):
        if n == heads // 2:
            rhs = jnp.concatenate([wk_ref[...], wv_ref[...]], axis=1)
        else:
            rhs = wq_ref[:, n * 256 : (n + 1) * 256]
        acc = jnp.dot(lhs, rhs, preferred_element_type=F32).astype(BF16)
        for i in range(count):
            for hh in range(2):
                head = 2 * n + hh
                outs[i // per][i % per, head * rows : (head + 1) * rows, :] = acc[
                    i * rows : (i + 1) * rows, hh * HD : (hh + 1) * HD
                ]
    for i in range(count):
        outs[i // per][i % per, (heads + 2) * rows :, :] = sq[first + i]


def project_first_body(rows, heads, gain_ref, wq_ref, wk_ref, wv_ref, *refs):
    blocks, outs, (hs, sq) = refs[:8], refs[8:12], refs[12:]
    y, c, z, x = place()
    gain = gain_ref[...].astype(F32).reshape(1, -1)
    depth = gain.shape[1]
    ones = jnp.ones((8, depth), BF16)
    pad = jnp.zeros((HD - rows, depth), BF16)
    for i, block in enumerate(blocks):
        for j in range(2):
            value = block[j * rows : (j + 1) * rows, :].astype(F32)
            dz = (y - i // 2 - z) % 4
            dx = (2 * (c ^ (i % 2)) + j - x) % 4
            e, f = jnp.where(c == 0, dx, dz), jnp.where(c == 0, dz, dx)
            slot = jnp.where(e == 2, f, 12 + f)
            slot = jnp.where(e == 1, jnp.where(f >= 2, 2 + f, 8 + f), slot)
            slot = jnp.where(e == 3, jnp.where(f < 2, 6 + f, 8 + f), slot)
            hs[slot] = (value * gain).astype(BF16)
            square = value * value
            high = square.astype(BF16)
            low = (square - high.astype(F32)).astype(BF16)
            total = jnp.zeros((8, HD), F32)
            for part in (high, low):
                total += lax.dot_general(
                    ones,
                    jnp.concatenate([part, pad], axis=0),
                    (((1,), (1,)), ((), ())),
                    preferred_element_type=F32,
                )
            sq[slot] = split_high_low(total)
    project_blocks(rows, heads, 0, hs, sq, wq_ref, wk_ref, wv_ref, outs)


def project_second_body(rows, heads, hs, sq, wq_ref, wk_ref, wv_ref, *outs):
    project_blocks(rows, heads, 8, hs, sq, wq_ref, wk_ref, wv_ref, outs)


def caches_body(after_ref, kc_hbm, vc_hbm, kc_ref, vc_ref, token_ref, sems):
    copies = [
        pltpu.make_async_copy(kc_hbm, kc_ref, sems.at[0]),
        pltpu.make_async_copy(vc_hbm, vc_ref, sems.at[1]),
    ]
    for copy in copies:
        copy.start()
    token_ref[...] = jnp.zeros_like(token_ref)
    for copy in copies:
        copy.wait()


def add_body(main, terms, *refs):
    ins, outs = refs[: len(refs) - len(terms)], refs[len(refs) - len(terms) :]
    for out, picks in zip(outs, terms):
        for i, pick in enumerate(picks):
            total = sum(ins[ref][block].astype(F32) for ref, block in pick)
            out[i, 0:main, :] = total[:main].astype(BF16)
            out[i, main:, :] = split_high_low(total[main : main + 8] + total[main + 8 :])


def attend_body(
    rows, heads, len_ref, p0_ref, p1_ref, p2_ref, r1_ref, r2_ref, r3_ref,
    cos_ref, sin_ref, kbuf, vbuf,
    ctx_ref, nk_ref, nv_ref, qs, os, kf, vf,
):
    seqs = rows // NEW
    slots = kbuf.shape[1]
    main = (heads + 2) * rows

    def total(lo, hi):
        refs = (p0_ref, p1_ref, p2_ref, r1_ref, r2_ref, r3_ref)
        return sum(ref[0, lo:hi, :].astype(F32) for ref in refs)

    square = total(main, main + 16)
    column = jnp.transpose(square[:8] + square[8:])[:rows, 0:1]
    scales = lax.rsqrt(column / D + EPSILON)
    cosine, sine = cos_ref[...], sin_ref[...]

    def rope(value):
        return value * cosine + pltpu.roll(value, HD // 2, 1) * sine

    for head in range(heads):
        value = total(head * rows, (head + 1) * rows) * scales
        qs[pl.ds(head, rows, stride=heads), :] = rope(value).astype(BF16).astype(F32)
    key = rope(total(heads * rows, (heads + 1) * rows) * scales).astype(BF16)
    nk_ref[...] = key
    kf[...] = key.astype(F32)
    fresh = (total((heads + 1) * rows, (heads + 2) * rows) * scales).astype(BF16)
    nv_ref[...] = fresh
    vf[...] = fresh.astype(F32)

    per = NEW * heads
    scale = HD ** (-0.5) * LOG2_E
    slot_of = lax.broadcasted_iota(jnp.int32, (1, slots), 1)
    second = lax.broadcasted_iota(jnp.int32, (per, 1), 0) >= heads

    def several(first, count):
        ids = [first + u for u in range(count)]
        query = [qs[pl.ds(pl.multiple_of(s * per, per), per), :] for s in ids]
        scores = [
            lax.dot_general(
                q.astype(BF16), kbuf[s], (((1,), (1,)), ((), ())), preferred_element_type=F32
            )
            for q, s in zip(query, ids)
        ]
        scores = [
            v + jnp.where(slot_of < len_ref[s], 0.0, -jnp.inf) for v, s in zip(scores, ids)
        ]
        s0 = [jnp.sum(q * kf[pl.ds(2 * s, 1), :], axis=1, keepdims=True) for q, s in zip(query, ids)]
        s1 = [
            jnp.where(
                second,
                jnp.sum(q * kf[pl.ds(2 * s + 1, 1), :], axis=1, keepdims=True),
                -jnp.inf,
            )
            for q, s in zip(query, ids)
        ]
        highest = [
            jnp.maximum(jnp.max(v, axis=1, keepdims=True), jnp.maximum(a, b))
            for v, a, b in zip(scores, s0, s1)
        ]
        probs = [jnp.exp2((v - m) * scale) for v, m in zip(scores, highest)]
        p0 = [jnp.exp2((v - m) * scale) for v, m in zip(s0, highest)]
        p1 = [jnp.exp2((v - m) * scale) for v, m in zip(s1, highest)]
        norm = [
            1.0 / (jnp.sum(v, axis=1, keepdims=True) + a + b) for v, a, b in zip(probs, p0, p1)
        ]
        out = [
            jnp.dot(v.astype(BF16), vbuf[s], preferred_element_type=F32)
            for v, s in zip(probs, ids)
        ]
        for u, s in enumerate(ids):
            w0, w1 = p0[u].astype(BF16).astype(F32), p1[u].astype(BF16).astype(F32)
            os[pl.ds(pl.multiple_of(s * per, per), per), :] = (
                out[u] + w0 * vf[pl.ds(2 * s, 1), :] + w1 * vf[pl.ds(2 * s + 1, 1), :]
            ) * norm[u]

    def step(i, carry):
        several(TOGETHER * i, TOGETHER)
        return carry

    lax.fori_loop(0, seqs // TOGETHER, step, 0)
    for head in range(heads):
        ctx_ref[:, head * HD : (head + 1) * HD] = os[pl.ds(head, rows, stride=heads), :].astype(BF16)


def output_body(a_ref, b_ref, w_ref, out_ref):
    lhs = jnp.concatenate([a_ref[...], b_ref[...]], axis=0)
    for n in range(w_ref.shape[1] // 256):
        cols = slice(n * 256, (n + 1) * 256)
        out_ref[:, cols] = jnp.dot(lhs, w_ref[:, cols], preferred_element_type=F32).astype(BF16)


def output_last_body(rows, a_ref, b_ref, w_ref, y0_ref, y1_ref, y3_ref, mine_ref, theirs_ref, y2):
    y, c, z, x = place()
    output_body(a_ref, b_ref, w_ref, y2)
    for f, source in enumerate((y0_ref, y1_ref, y2, y3_ref)):
        for e in range(4):
            zz = jnp.where(c == 0, z - f, z - e) % 4
            xx = jnp.where(c == 0, x - e, x - f) % 4
            slot = 2 * ((zz - y) % 4) + xx % 2
            top = e * rows
            own = xx // 2 == c

            @pl.when(own)
            def _(slot=slot, source=source, top=top):
                mine_ref[slot] = source[top : top + rows, :]

            @pl.when(jnp.logical_not(own))
            def _(slot=slot, source=source, top=top):
                theirs_ref[slot] = source[top : top + rows, :]


def local(hidden, gain, w_query, w_key, w_value, w_out, key_cache, value_cache, lengths):
    heads = w_query.shape[1] // HD
    depth = hidden.shape[1]
    width = w_out.shape[1]
    rows = key_cache.shape[0] * NEW
    main = (heads + 2) * rows
    length = main + 16

    positions = (lengths[:, None] + jnp.arange(NEW, dtype=jnp.int32)[None, :]).reshape(-1)
    indices = jnp.arange(HD // 2, dtype=F32)
    inverse = jnp.power(F32(ROPE_BASE), -2.0 * indices / HD)
    angles = positions.astype(F32)[:, None] * inverse[None, :]
    cosine, sine = jnp.cos(angles), jnp.sin(angles)
    cosine = jnp.concatenate([cosine, cosine], 1)
    sine = jnp.concatenate([-sine, sine], 1)

    two, one, three = [shift_y(hidden, d) for d in (2, 1, 3)]
    received = [one, two, three]
    sources = [hidden, gain, w_query, w_key, w_value]
    back, own, scale, *weights = call(
        load_body,
        [pltpu.VMEM(v.shape, v.dtype) for v in [received[0]] + sources],
        [VSPEC] + [HSPEC] * 5,
        "load",
        4,
        scratch=[pltpu.SemaphoreType.DMA((6,))],
    )(received[0], *[in_hbm(v) for v in sources])
    blocks = [own, swap_core(hidden)]
    for value in [back] + received[1:]:
        blocks += [value, swap_core(value)]

    half = shape((2, length, HD))
    two_a, two_b, one_b, three_a, scaled, squares = call(
        functools.partial(project_first_body, rows, heads),
        [half] * 4 + [shape((16, rows, depth)), shape((16, 16, HD))],
        [VSPEC] * 12,
        "project_first",
        14,
    )(scale, *weights, *blocks)
    over_a, over_b = shift_first(two_a, 1), shift_first(two_b, 3)
    from_one_b, from_three_a = shift_first(one_b, 1), shift_first(three_a, 3)
    one_a, three_b, own_a, own_b = call(
        functools.partial(project_second_body, rows, heads),
        [half] * 4,
        [VSPEC] * 5,
        "project_second",
        12,
    )(scaled, squares, *weights)

    def add(terms, *values):
        return call(
            functools.partial(add_body, main, terms),
            [shape((len(picks), length, HD)) for picks in terms],
            [VSPEC] * len(values),
            "add",
            8,
        )(*values)

    pairwise = [[[(0, 0), (1, 0)], [(0, 1), (1, 1)]]]
    sum_one, sum_three = add(pairwise, one_a, over_a)[0], add(pairwise, three_b, over_b)[0]
    from_one_a, from_three_b = shift_first(sum_one, 1), shift_first(sum_three, 3)
    keys, values, token = call(
        caches_body,
        [pltpu.VMEM(v.shape, v.dtype) for v in (key_cache, value_cache)] + [shape((16, HD))],
        [VSPEC, HSPEC, HSPEC],
        "load_caches",
        4,
        scratch=[pltpu.SemaphoreType.DMA((2,))],
    )(sum_three, in_hbm(key_cache), in_hbm(value_cache))
    terms = [
        [[(1, 0), (4, 0), (5, 0)]],
        [[(0, 1), (2, 1), (3, 1)]],
        [[(1, 1), (4, 1), (5, 1)]],
    ]
    two, one, three = add(
        terms, own_a, own_b, from_one_a, from_three_a, from_one_b, from_three_b, token
    )
    arrived = [shift_second(two, 2), shift_second(one, 1), shift_second(three, 3)]
    parts = [own_a, from_one_a, from_three_a] + arrived

    context, fresh_keys, fresh_values = call(
        functools.partial(attend_body, rows, heads),
        [shape((rows, heads * HD)), shape((rows, HD)), shape((rows, HD))],
        [SSPEC] + [VSPEC] * 10,
        "attend",
        10,
        scratch=[
            pltpu.VMEM((rows * heads, HD), F32),
            pltpu.VMEM((rows * heads, HD), F32),
            pltpu.VMEM((rows, HD), F32),
            pltpu.VMEM((rows, HD), F32),
        ],
    )(lengths, *parts, cosine, sine, keys, values)

    two, one, three = [shift_first(context, e) for e in (2, 1, 3)]
    low, high = jnp.concatenate([context, one], 0), jnp.concatenate([two, three], 0)
    one_low, three_high = shift_second(low, 1), shift_second(high, 3)
    two_low, two_high = shift_second(one_low, 1), shift_second(three_high, 3)
    one_high, three_low = shift_second(high, 1), shift_second(low, 3)

    def project_out(a, b):
        return call(
            output_body,
            [shape((4 * rows, width))],
            [VSPEC] * 3,
            "project_out",
            8,
        )(a, b, w_out)[0]

    mine, theirs = call(
        functools.partial(output_last_body, rows),
        [shape((8, rows, width)), shape((8, rows, width))],
        [VSPEC] * 6,
        "project_out_last",
        12,
        scratch=[pltpu.VMEM((4 * rows, width), BF16)],
    )(
        two_low,
        two_high,
        w_out,
        project_out(low, high),
        project_out(one_low, one_high),
        project_out(three_low, three_high),
    )
    both = mine.astype(F32) + swap_core(theirs).astype(F32)
    over_a, over_b = shift_y(both[4].astype(BF16), 1), shift_y(both[5].astype(BF16), 3)
    from_one_b, from_three_a = shift_y(both[3].astype(BF16), 1), shift_y(both[6].astype(BF16), 3)
    from_one_a = shift_y((both[2] + over_a.astype(F32)).astype(BF16), 1)
    from_three_b = shift_y((both[7] + over_b.astype(F32)).astype(BF16), 3)
    upper = both[0] + from_one_a.astype(F32) + from_three_a.astype(F32)
    lower = both[1] + from_one_b.astype(F32) + from_three_b.astype(F32)
    result = hidden.astype(F32) + jnp.concatenate([upper, lower], axis=0)
    return result.astype(BF16), fresh_keys, fresh_values


def solution(mesh):
    return jax.shard_map(
        local,
        mesh=mesh,
        in_specs=(
            P("gx", "gy"),
            P("gy"),
            P("gy", "gx"),
            P("gy", "gx"),
            P("gy", "gx"),
            P("gx", "gy"),
            P("gy", None, "gx"),
            P("gy", None, "gx"),
            P("gy"),
        ),
        out_specs=(P("gx", "gy"), P("gy", "gx"), P("gy", "gx")),
        check_vma=False,
    )
```

```python
import functools

import jax
import jax.numpy as jnp
from jax import lax
from jax.experimental import pallas as pl
from jax.experimental.pallas import tpu as pltpu
from jax.sharding import PartitionSpec as P

D = 16384
HD = 128
NEW = 2
EPSILON = 1e-05
ROPE_BASE = 500000.0

NY = NZ = NX = 4
NC = 2
AXES = ("gx", "gy")
BF16 = jnp.bfloat16
F32 = jnp.float32
MIB = 1024 * 1024
TOGETHER = 8
LOG2_E = 1.4426950408889634


def pairs(move):
    out = []
    for y in range(NY):
        for c in range(NC):
            for z in range(NZ):
                for x in range(NX):
                    y2, c2, z2, x2 = move(y, c, z, x)
                    source = ((y * NC + c) * NZ + z) * NX + x
                    target = (((y2 % NY) * NC + c2 % NC) * NZ + z2 % NZ) * NX + x2 % NX
                    out.append((source, target))
    return out


def swap_core(value):
    return lax.ppermute(value, AXES, pairs(lambda y, c, z, x: (y, c + 1, z, x)))


def shift_y(value, step):
    return lax.ppermute(value, AXES, pairs(lambda y, c, z, x: (y + step, c, z, x)))


def shift_first(value, step):
    def move(y, c, z, x):
        return (y, c, z, x + step) if c == 0 else (y, c, z + step, x)

    return lax.ppermute(value, AXES, pairs(move))


def shift_second(value, step):
    def move(y, c, z, x):
        return (y, c, z + step, x) if c == 0 else (y, c, z, x + step)

    return lax.ppermute(value, AXES, pairs(move))


VSPEC = pl.BlockSpec(memory_space=pltpu.VMEM)
SSPEC = pl.BlockSpec(memory_space=pltpu.SMEM)
HSPEC = pl.BlockSpec(memory_space=pltpu.HBM)


def call(body, outs, in_specs, name, vmem, scratch=(), flops=0, moved=0):
    return pl.pallas_call(
        body,
        out_shape=outs,
        in_specs=in_specs,
        out_specs=[VSPEC] * len(outs),
        scratch_shapes=list(scratch),
        compiler_params=pltpu.CompilerParams(vmem_limit_bytes=vmem * MIB),
        cost_estimate=pl.CostEstimate(flops=flops, bytes_accessed=moved, transcendentals=0),
        name=name,
    )


def shape(dims, dtype=BF16):
    return jax.ShapeDtypeStruct(dims, dtype)


def in_hbm(value):
    return pltpu.with_memory_space_constraint(value, pltpu.HBM)


def place():
    gx, gy = lax.axis_index("gx"), lax.axis_index("gy")
    return gx // NC, gx % NC, gy // NX, gy % NX


def split_high_low(total):
    high = total.astype(BF16).astype(F32)
    return jnp.concatenate([high, total - high], axis=0).astype(BF16)


def load_body(back_ref, hidden_hbm, gain_hbm, wq_hbm, wk_hbm, wv_hbm, *refs):
    outs, sems = refs[:-1], refs[-1]
    sources = (back_ref, hidden_hbm, gain_hbm, wq_hbm, wk_hbm, wv_hbm)
    copies = [
        pltpu.make_async_copy(source, out, sems.at[i])
        for i, (source, out) in enumerate(zip(sources, outs))
    ]
    for copy in copies:
        copy.start()
    for copy in copies:
        copy.wait()


def project_blocks(rows, heads, first, hs, sq, wq_ref, wk_ref, wv_ref, outs):
    per = outs[0].shape[0]
    count = per * len(outs)
    lhs = hs[first : first + count].reshape(count * rows, hs.shape[2])
    for n in range(heads // 2 + 1):
        if n == heads // 2:
            rhs = jnp.concatenate([wk_ref[...], wv_ref[...]], axis=1)
        else:
            rhs = wq_ref[:, n * 256 : (n + 1) * 256]
        acc = jnp.dot(lhs, rhs, preferred_element_type=F32).astype(BF16)
        for i in range(count):
            for hh in range(2):
                head = 2 * n + hh
                outs[i // per][i % per, head * rows : (head + 1) * rows, :] = acc[
                    i * rows : (i + 1) * rows, hh * HD : (hh + 1) * HD
                ]
    for i in range(count):
        outs[i // per][i % per, (heads + 2) * rows :, :] = sq[first + i]


def project_first_body(rows, heads, gain_ref, wq_ref, wk_ref, wv_ref, *refs):
    blocks, outs, (hs, sq) = refs[:8], refs[8:12], refs[12:]
    y, c, z, x = place()
    gain = gain_ref[...].astype(F32).reshape(1, -1)
    depth = gain.shape[1]
    pad = jnp.zeros((HD - rows, HD), F32)
    for i, block in enumerate(blocks):
        for j in range(2):
            value = block[j * rows : (j + 1) * rows, :].astype(F32)
            dz = (y - i // 2 - z) % 4
            dx = (2 * (c ^ (i % 2)) + j - x) % 4
            e, f = jnp.where(c == 0, dx, dz), jnp.where(c == 0, dz, dx)
            slot = jnp.where(e == 2, f, 12 + f)
            slot = jnp.where(e == 1, jnp.where(f >= 2, 2 + f, 8 + f), slot)
            slot = jnp.where(e == 3, jnp.where(f < 2, 6 + f, 8 + f), slot)
            hs[slot] = (value * gain).astype(BF16)
            part = sum(value[:, n : n + HD] * value[:, n : n + HD] for n in range(0, depth, HD))
            turned = jnp.transpose(jnp.concatenate([part, pad], axis=0))
            total = jnp.broadcast_to(jnp.sum(turned, axis=0, keepdims=True), (8, HD))
            sq[slot] = split_high_low(total)
    project_blocks(rows, heads, 0, hs, sq, wq_ref, wk_ref, wv_ref, outs)


def project_second_body(rows, heads, hs, sq, wq_ref, wk_ref, wv_ref, *outs):
    project_blocks(rows, heads, 8, hs, sq, wq_ref, wk_ref, wv_ref, outs)


def caches_body(after_ref, kc_hbm, vc_hbm, kc_ref, vc_ref, token_ref, sems):
    copies = [
        pltpu.make_async_copy(kc_hbm, kc_ref, sems.at[0]),
        pltpu.make_async_copy(vc_hbm, vc_ref, sems.at[1]),
    ]
    for copy in copies:
        copy.start()
    token_ref[...] = jnp.zeros_like(token_ref)
    for copy in copies:
        copy.wait()


def add_body(main, terms, *refs):
    ins, outs = refs[: len(refs) - len(terms)], refs[len(refs) - len(terms) :]
    for out, picks in zip(outs, terms):
        for i, pick in enumerate(picks):
            total = sum(ins[ref][block].astype(F32) for ref, block in pick)
            out[i, 0:main, :] = total[:main].astype(BF16)
            out[i, main:, :] = split_high_low(total[main : main + 8] + total[main + 8 :])


def attend_body(
    rows, heads, len_ref, p0_ref, p1_ref, p2_ref, r1_ref, r2_ref, r3_ref,
    cos_ref, sin_ref, kbuf, vbuf,
    ctx_ref, nk_ref, nv_ref, qs, os, kf, vf,
):
    seqs = rows // NEW
    slots = kbuf.shape[1]
    main = (heads + 2) * rows

    def total(lo, hi):
        refs = (p0_ref, p1_ref, p2_ref, r1_ref, r2_ref, r3_ref)
        return sum(ref[0, lo:hi, :].astype(F32) for ref in refs)

    square = total(main, main + 16)
    column = jnp.transpose(square[:8] + square[8:])[:rows, 0:1]
    scales = lax.rsqrt(column / D + EPSILON)
    cosine, sine = cos_ref[...], sin_ref[...]

    def rope(value):
        return value * cosine + pltpu.roll(value, HD // 2, 1) * sine

    for head in range(heads):
        value = total(head * rows, (head + 1) * rows) * scales
        qs[pl.ds(head, rows, stride=heads), :] = rope(value).astype(BF16).astype(F32)
    key = rope(total(heads * rows, (heads + 1) * rows) * scales).astype(BF16)
    nk_ref[...] = key
    kf[...] = key.astype(F32)
    fresh = (total((heads + 1) * rows, (heads + 2) * rows) * scales).astype(BF16)
    nv_ref[...] = fresh
    vf[...] = fresh.astype(F32)

    per = NEW * heads
    scale = HD ** (-0.5) * LOG2_E
    slot_of = lax.broadcasted_iota(jnp.int32, (1, slots), 1)
    second = lax.broadcasted_iota(jnp.int32, (per, 1), 0) >= heads

    def several(first, count):
        ids = [first + u for u in range(count)]
        query = [qs[pl.ds(pl.multiple_of(s * per, per), per), :] for s in ids]
        scores = [
            lax.dot_general(
                q.astype(BF16), kbuf[s], (((1,), (1,)), ((), ())), preferred_element_type=F32
            )
            for q, s in zip(query, ids)
        ]
        scores = [
            v + jnp.where(slot_of < len_ref[s], 0.0, -jnp.inf) for v, s in zip(scores, ids)
        ]
        s0 = [jnp.sum(q * kf[pl.ds(2 * s, 1), :], axis=1, keepdims=True) for q, s in zip(query, ids)]
        s1 = [
            jnp.where(
                second,
                jnp.sum(q * kf[pl.ds(2 * s + 1, 1), :], axis=1, keepdims=True),
                -jnp.inf,
            )
            for q, s in zip(query, ids)
        ]
        highest = [
            jnp.maximum(jnp.max(v, axis=1, keepdims=True), jnp.maximum(a, b))
            for v, a, b in zip(scores, s0, s1)
        ]
        probs = [jnp.exp2((v - m) * scale) for v, m in zip(scores, highest)]
        p0 = [jnp.exp2((v - m) * scale) for v, m in zip(s0, highest)]
        p1 = [jnp.exp2((v - m) * scale) for v, m in zip(s1, highest)]
        norm = [
            1.0 / (jnp.sum(v, axis=1, keepdims=True) + a + b) for v, a, b in zip(probs, p0, p1)
        ]
        out = [
            jnp.dot(v.astype(BF16), vbuf[s], preferred_element_type=F32)
            for v, s in zip(probs, ids)
        ]
        for u, s in enumerate(ids):
            w0, w1 = p0[u].astype(BF16).astype(F32), p1[u].astype(BF16).astype(F32)
            os[pl.ds(pl.multiple_of(s * per, per), per), :] = (
                out[u] + w0 * vf[pl.ds(2 * s, 1), :] + w1 * vf[pl.ds(2 * s + 1, 1), :]
            ) * norm[u]

    def step(i, carry):
        several(TOGETHER * i, TOGETHER)
        return carry

    lax.fori_loop(0, seqs // TOGETHER, step, 0)
    for head in range(heads):
        ctx_ref[:, head * HD : (head + 1) * HD] = os[pl.ds(head, rows, stride=heads), :].astype(BF16)


def together_body(token_ref, a_ref, out_ref):
    out_ref[...] = a_ref[...]


def output_body(a_ref, b_ref, w_ref, out_ref):
    lhs = jnp.concatenate([a_ref[...], b_ref[...]], axis=0)
    for n in range(w_ref.shape[1] // 256):
        cols = slice(n * 256, (n + 1) * 256)
        out_ref[:, cols] = jnp.dot(lhs, w_ref[:, cols], preferred_element_type=F32).astype(BF16)


def output_last_body(rows, a_ref, b_ref, w_ref, y0_ref, y1_ref, y3_ref, mine_ref, theirs_ref, y2):
    y, c, z, x = place()
    output_body(a_ref, b_ref, w_ref, y2)
    for f, source in enumerate((y0_ref, y1_ref, y2, y3_ref)):
        for place_of, e in enumerate((0, 2, 1, 3)):
            zz = jnp.where(c == 0, z - f, z - e) % 4
            xx = jnp.where(c == 0, x - e, x - f) % 4
            slot = 2 * ((zz - y) % 4) + xx % 2
            top = place_of * rows
            own = xx // 2 == c

            @pl.when(own)
            def _(slot=slot, source=source, top=top):
                mine_ref[slot] = source[top : top + rows, :]

            @pl.when(jnp.logical_not(own))
            def _(slot=slot, source=source, top=top):
                theirs_ref[slot] = source[top : top + rows, :]


def local(hidden, gain, w_query, w_key, w_value, w_out, key_cache, value_cache, lengths):
    heads = w_query.shape[1] // HD
    depth = hidden.shape[1]
    width = w_out.shape[1]
    rows = key_cache.shape[0] * NEW
    main = (heads + 2) * rows
    length = main + 16

    positions = (lengths[:, None] + jnp.arange(NEW, dtype=jnp.int32)[None, :]).reshape(-1)
    indices = jnp.arange(HD // 2, dtype=F32)
    inverse = jnp.power(F32(ROPE_BASE), -2.0 * indices / HD)
    angles = positions.astype(F32)[:, None] * inverse[None, :]
    cosine, sine = jnp.cos(angles), jnp.sin(angles)
    cosine = jnp.concatenate([cosine, cosine], 1)
    sine = jnp.concatenate([-sine, sine], 1)

    two, one, three = [shift_y(hidden, d) for d in (2, 1, 3)]
    received = [one, two, three]
    sources = [hidden, gain, w_query, w_key, w_value]
    back, own, scale, *weights = call(
        load_body,
        [pltpu.VMEM(v.shape, v.dtype) for v in [received[0]] + sources],
        [VSPEC] + [HSPEC] * 5,
        "load",
        4,
        scratch=[pltpu.SemaphoreType.DMA((6,))],
    )(received[0], *[in_hbm(v) for v in sources])
    blocks = [own, swap_core(hidden)]
    for value in [back] + received[1:]:
        blocks += [value, swap_core(value)]

    half = shape((2, length, HD))
    two_a, two_b, one_b, three_a, scaled, squares = call(
        functools.partial(project_first_body, rows, heads),
        [half] * 4 + [shape((16, rows, depth)), shape((16, 16, HD))],
        [VSPEC] * 12,
        "project_first",
        14,
    )(scale, *weights, *blocks)
    over_a, over_b = shift_first(two_a, 1), shift_first(two_b, 3)
    from_one_b, from_three_a = shift_first(one_b, 1), shift_first(three_a, 3)
    one_a, three_b, own_a, own_b = call(
        functools.partial(project_second_body, rows, heads),
        [half] * 4,
        [VSPEC] * 5,
        "project_second",
        12,
    )(scaled, squares, *weights)

    def add(terms, *values):
        return call(
            functools.partial(add_body, main, terms),
            [shape((len(picks), length, HD)) for picks in terms],
            [VSPEC] * len(values),
            "add",
            8,
        )(*values)

    pairwise = [[[(0, 0), (1, 0)], [(0, 1), (1, 1)]]]
    sum_one, sum_three = add(pairwise, one_a, over_a)[0], add(pairwise, three_b, over_b)[0]
    from_one_a, from_three_b = shift_first(sum_one, 1), shift_first(sum_three, 3)
    keys, values, token = call(
        caches_body,
        [pltpu.VMEM(v.shape, v.dtype) for v in (key_cache, value_cache)] + [shape((16, HD))],
        [VSPEC, HSPEC, HSPEC],
        "load_caches",
        4,
        scratch=[pltpu.SemaphoreType.DMA((2,))],
    )(sum_three, in_hbm(key_cache), in_hbm(value_cache))
    terms = [
        [[(1, 0), (4, 0), (5, 0)]],
        [[(0, 1), (2, 1), (3, 1)]],
        [[(1, 1), (4, 1), (5, 1)]],
    ]
    two, one, three = add(
        terms, own_a, own_b, from_one_a, from_three_a, from_one_b, from_three_b, token
    )
    arrived = [shift_second(two, 2), shift_second(one, 1), shift_second(three, 3)]
    parts = [own_a, from_one_a, from_three_a] + arrived

    context, fresh_keys, fresh_values = call(
        functools.partial(attend_body, rows, heads),
        [shape((rows, heads * HD)), shape((rows, HD)), shape((rows, HD))],
        [SSPEC] + [VSPEC] * 10,
        "attend",
        10,
        scratch=[
            pltpu.VMEM((rows * heads, HD), F32),
            pltpu.VMEM((rows * heads, HD), F32),
            pltpu.VMEM((rows, HD), F32),
            pltpu.VMEM((rows, HD), F32),
        ],
    )(lengths, *parts, cosine, sine, keys, values)

    context = call(
        together_body,
        [shape(context.shape)],
        [VSPEC] * 2,
        "together",
        4,
    )(swap_core(fresh_keys), context)[0]
    two, one, three = [shift_first(context, e) for e in (2, 1, 3)]
    low, high = jnp.concatenate([context, two], 0), jnp.concatenate([one, three], 0)
    one_low, three_high = shift_second(low, 1), shift_second(high, 3)
    two_low, two_high = shift_second(one_low, 1), shift_second(three_high, 3)
    one_high, three_low = shift_second(high, 1), shift_second(low, 3)

    def project_out(a, b):
        return call(
            output_body,
            [shape((4 * rows, width))],
            [VSPEC] * 3,
            "project_out",
            8,
        )(a, b, w_out)[0]

    mine, theirs = call(
        functools.partial(output_last_body, rows),
        [shape((8, rows, width)), shape((8, rows, width))],
        [VSPEC] * 6,
        "project_out_last",
        12,
        scratch=[pltpu.VMEM((4 * rows, width), BF16)],
    )(
        two_low,
        two_high,
        w_out,
        project_out(low, high),
        project_out(one_low, one_high),
        project_out(three_low, three_high),
    )
    both = mine.astype(F32) + swap_core(theirs).astype(F32)
    over_a, over_b = shift_y(both[4].astype(BF16), 1), shift_y(both[5].astype(BF16), 3)
    from_one_b, from_three_a = shift_y(both[3].astype(BF16), 1), shift_y(both[6].astype(BF16), 3)
    from_one_a = shift_y((both[2] + over_a.astype(F32)).astype(BF16), 1)
    from_three_b = shift_y((both[7] + over_b.astype(F32)).astype(BF16), 3)
    upper = both[0] + from_one_a.astype(F32) + from_three_a.astype(F32)
    lower = both[1] + from_one_b.astype(F32) + from_three_b.astype(F32)
    result = hidden.astype(F32) + jnp.concatenate([upper, lower], axis=0)
    return result.astype(BF16), fresh_keys, fresh_values


def solution(mesh):
    return jax.shard_map(
        local,
        mesh=mesh,
        in_specs=(
            P("gx", "gy"),
            P("gy"),
            P("gy", "gx"),
            P("gy", "gx"),
            P("gy", "gx"),
            P("gx", "gy"),
            P("gy", None, "gx"),
            P("gy", None, "gx"),
            P("gy"),
        ),
        out_specs=(P("gx", "gy"), P("gy", "gx"), P("gy", "gx")),
        check_vma=False,
    )
```

```python
import functools

import jax
import jax.numpy as jnp
from jax import lax
from jax.experimental import pallas as pl
from jax.experimental.pallas import tpu as pltpu
from jax.sharding import PartitionSpec as P

D = 16384
HD = 128
NEW = 2
EPSILON = 1e-05
ROPE_BASE = 500000.0

NY = NZ = NX = 4
NC = 2
AXES = ("gx", "gy")
BF16 = jnp.bfloat16
F32 = jnp.float32
MIB = 1024 * 1024
TOGETHER = 8
STEP = 64
LOG2_E = 1.4426950408889634


def pairs(move):
    out = []
    for y in range(NY):
        for c in range(NC):
            for z in range(NZ):
                for x in range(NX):
                    y2, c2, z2, x2 = move(y, c, z, x)
                    source = ((y * NC + c) * NZ + z) * NX + x
                    target = (((y2 % NY) * NC + c2 % NC) * NZ + z2 % NZ) * NX + x2 % NX
                    out.append((source, target))
    return out


def swap_core(value):
    return lax.ppermute(value, AXES, pairs(lambda y, c, z, x: (y, c + 1, z, x)))


def shift_y(value, step):
    return lax.ppermute(value, AXES, pairs(lambda y, c, z, x: (y + step, c, z, x)))


def shift_first(value, step):
    def move(y, c, z, x):
        return (y, c, z, x + step) if c == 0 else (y, c, z + step, x)

    return lax.ppermute(value, AXES, pairs(move))


def shift_second(value, step):
    def move(y, c, z, x):
        return (y, c, z + step, x) if c == 0 else (y, c, z, x + step)

    return lax.ppermute(value, AXES, pairs(move))


VSPEC = pl.BlockSpec(memory_space=pltpu.VMEM)
SSPEC = pl.BlockSpec(memory_space=pltpu.SMEM)
HSPEC = pl.BlockSpec(memory_space=pltpu.HBM)


def call(body, outs, in_specs, name, vmem, scratch=(), aliases={}):
    return pl.pallas_call(
        body,
        out_shape=outs,
        in_specs=in_specs,
        out_specs=[VSPEC] * len(outs),
        scratch_shapes=list(scratch),
        compiler_params=pltpu.CompilerParams(vmem_limit_bytes=vmem * MIB),
        cost_estimate=pl.CostEstimate(flops=0, bytes_accessed=0, transcendentals=0),
        input_output_aliases=aliases,
        name=name,
    )


def shape(dims, dtype=BF16):
    return jax.ShapeDtypeStruct(dims, dtype)


def in_hbm(value):
    return pltpu.with_memory_space_constraint(value, pltpu.HBM)


def place():
    gx, gy = lax.axis_index("gx"), lax.axis_index("gy")
    return gx // NC, gx % NC, gy // NX, gy % NX


def split_high_low(total):
    high = total.astype(BF16).astype(F32)
    return jnp.concatenate([high, total - high], axis=0).astype(BF16)


def load_body(back_ref, hidden_hbm, gain_hbm, wq_hbm, wk_hbm, wv_hbm, *refs):
    outs, sems = refs[:-1], refs[-1]
    sources = (back_ref, hidden_hbm, gain_hbm, wq_hbm, wk_hbm, wv_hbm)
    copies = [
        pltpu.make_async_copy(source, out, sems.at[i])
        for i, (source, out) in enumerate(zip(sources, outs))
    ]
    for copy in copies:
        copy.start()
    for copy in copies:
        copy.wait()


def project_blocks(rows, heads, first, hs, sq, wq_ref, wk_ref, wv_ref, outs):
    per = outs[0].shape[0]
    count = per * len(outs)
    lhs = hs[first : first + count].reshape(count * rows, hs.shape[2])
    for n in range(heads // 2 + 1):
        if n == heads // 2:
            rhs = jnp.concatenate([wk_ref[...], wv_ref[...]], axis=1)
        else:
            rhs = wq_ref[:, n * 256 : (n + 1) * 256]
        acc = jnp.dot(lhs, rhs, preferred_element_type=F32).astype(BF16)
        for i in range(count):
            for hh in range(2):
                head = 2 * n + hh
                outs[i // per][i % per, head * rows : (head + 1) * rows, :] = acc[
                    i * rows : (i + 1) * rows, hh * HD : (hh + 1) * HD
                ]
    for i in range(count):
        outs[i // per][i % per, (heads + 2) * rows :, :] = sq[first + i]


def project_first_body(rows, heads, gain_ref, wq_ref, wk_ref, wv_ref, *refs):
    blocks, outs, (hs, sq) = refs[:8], refs[8:12], refs[12:]
    y, c, z, x = place()
    gain = gain_ref[...].astype(F32).reshape(1, -1)
    depth = gain.shape[1]
    pad = jnp.zeros((HD - rows, HD), F32)
    for i, block in enumerate(blocks):
        for j in range(2):
            dz = (y - i // 2 - z) % 4
            dx = (2 * (c ^ (i % 2)) + j - x) % 4
            e, f = jnp.where(c == 0, dx, dz), jnp.where(c == 0, dz, dx)
            slot = jnp.where(e == 2, f, 12 + f)
            slot = jnp.where(e == 1, jnp.where(f >= 2, 2 + f, 8 + f), slot)
            slot = jnp.where(e == 3, jnp.where(f < 2, 6 + f, 8 + f), slot)
            parts = []
            for top in range(0, rows, 16):
                value = block[j * rows + top : j * rows + top + 16, :].astype(F32)
                hs[slot, top : top + 16, :] = (value * gain).astype(BF16)
                parts.append(
                    sum(value[:, n : n + HD] * value[:, n : n + HD] for n in range(0, depth, HD))
                )
            turned = jnp.transpose(jnp.concatenate(parts + [pad], axis=0))
            total = jnp.broadcast_to(jnp.sum(turned, axis=0, keepdims=True), (8, HD))
            sq[slot] = split_high_low(total)
    project_blocks(rows, heads, 0, hs, sq, wq_ref, wk_ref, wv_ref, outs)


def project_second_body(rows, heads, hs, sq, wq_ref, wk_ref, wv_ref, *outs):
    project_blocks(rows, heads, 8, hs, sq, wq_ref, wk_ref, wv_ref, outs)


def caches_body(after_ref, kc_hbm, vc_hbm, kc_ref, vc_ref, token_ref, sems):
    copies = [
        pltpu.make_async_copy(kc_hbm, kc_ref, sems.at[0]),
        pltpu.make_async_copy(vc_hbm, vc_ref, sems.at[1]),
    ]
    for copy in copies:
        copy.start()
    token_ref[...] = jnp.zeros_like(token_ref)
    for copy in copies:
        copy.wait()


def add_body(main, terms, *refs):
    ins, outs = refs[: len(refs) - len(terms)], refs[len(refs) - len(terms) :]
    for out, picks in zip(outs, terms):
        for i, pick in enumerate(picks):
            for top in range(0, main, STEP):
                total = sum(ins[ref][block, top : top + STEP, :].astype(F32) for ref, block in pick)
                out[i, top : top + STEP, :] = total.astype(BF16)
            total = sum(ins[ref][block, main:, :].astype(F32) for ref, block in pick)
            out[i, main:, :] = split_high_low(total[:8] + total[8:])


def early_sum_body(picks, *refs):
    ins, outs = refs[:4], refs[4:]
    for (out, at), pick in zip(((outs[0], 0), (outs[1], 0), (outs[1], 1), (outs[1], 2)), picks):
        out[at] = sum(ins[ref][block].astype(F32) for ref, block in pick)


def attend_body(
    rows, heads, len_ref, p0_ref, p1_ref, r1_ref, r2_ref, r3_ref,
    cos_ref, sin_ref, kbuf, vbuf,
    ctx_ref, nk_ref, nv_ref, qs, os, kf, vf,
):
    seqs = rows // NEW
    slots = kbuf.shape[1]
    main = (heads + 2) * rows

    def total(lo, hi):
        refs = (p0_ref, p1_ref, r1_ref, r2_ref, r3_ref)
        return sum(ref[0, lo:hi, :].astype(F32) for ref in refs)

    square = total(main, main + 16)
    column = jnp.transpose(square[:8] + square[8:])[:rows, 0:1]
    scales = lax.rsqrt(column / D + EPSILON)
    cosine, sine = cos_ref[...], sin_ref[...]

    def rope(value):
        return value * cosine + pltpu.roll(value, HD // 2, 1) * sine

    for head in range(heads):
        value = total(head * rows, (head + 1) * rows) * scales
        qs[pl.ds(head, rows, stride=heads), :] = rope(value).astype(BF16).astype(F32)
    key = rope(total(heads * rows, (heads + 1) * rows) * scales).astype(BF16)
    nk_ref[...] = key
    kf[...] = key.astype(F32)
    fresh = (total((heads + 1) * rows, (heads + 2) * rows) * scales).astype(BF16)
    nv_ref[...] = fresh
    vf[...] = fresh.astype(F32)

    per = NEW * heads
    scale = HD ** (-0.5) * LOG2_E
    slot_of = lax.broadcasted_iota(jnp.int32, (1, slots), 1)
    second = lax.broadcasted_iota(jnp.int32, (per, 1), 0) >= heads

    def several(first, count):
        ids = [first + u for u in range(count)]
        query = [qs[pl.ds(pl.multiple_of(s * per, per), per), :] for s in ids]
        scores = [
            lax.dot_general(
                q.astype(BF16), kbuf[s], (((1,), (1,)), ((), ())), preferred_element_type=F32
            )
            for q, s in zip(query, ids)
        ]
        scores = [
            v + jnp.where(slot_of < len_ref[s], 0.0, -jnp.inf) for v, s in zip(scores, ids)
        ]
        s0 = [jnp.sum(q * kf[pl.ds(2 * s, 1), :], axis=1, keepdims=True) for q, s in zip(query, ids)]
        s1 = [
            jnp.where(
                second,
                jnp.sum(q * kf[pl.ds(2 * s + 1, 1), :], axis=1, keepdims=True),
                -jnp.inf,
            )
            for q, s in zip(query, ids)
        ]
        highest = [
            jnp.maximum(jnp.max(v, axis=1, keepdims=True), jnp.maximum(a, b))
            for v, a, b in zip(scores, s0, s1)
        ]
        probs = [jnp.exp2((v - m) * scale) for v, m in zip(scores, highest)]
        p0 = [jnp.exp2((v - m) * scale) for v, m in zip(s0, highest)]
        p1 = [jnp.exp2((v - m) * scale) for v, m in zip(s1, highest)]
        norm = [
            1.0 / (jnp.sum(v, axis=1, keepdims=True) + a + b) for v, a, b in zip(probs, p0, p1)
        ]
        out = [
            jnp.dot(v.astype(BF16), vbuf[s], preferred_element_type=F32)
            for v, s in zip(probs, ids)
        ]
        for u, s in enumerate(ids):
            w0, w1 = p0[u].astype(BF16).astype(F32), p1[u].astype(BF16).astype(F32)
            os[pl.ds(pl.multiple_of(s * per, per), per), :] = (
                out[u] + w0 * vf[pl.ds(2 * s, 1), :] + w1 * vf[pl.ds(2 * s + 1, 1), :]
            ) * norm[u]

    def step(i, carry):
        several(TOGETHER * i, TOGETHER)
        return carry

    lax.fori_loop(0, seqs // TOGETHER, step, 0)
    for head in range(heads):
        ctx_ref[:, head * HD : (head + 1) * HD] = os[pl.ds(head, rows, stride=heads), :].astype(BF16)


def together_body(token_ref, a_ref, out_ref):
    out_ref[...] = a_ref[...]


def output_body(a_ref, b_ref, w_ref, out_ref):
    lhs = jnp.concatenate([a_ref[...], b_ref[...]], axis=0)
    for n in range(w_ref.shape[1] // 256):
        cols = slice(n * 256, (n + 1) * 256)
        out_ref[:, cols] = jnp.dot(lhs, w_ref[:, cols], preferred_element_type=F32).astype(BF16)


def arrange(rows, f, source, mine_ref, theirs_ref):
    y, c, z, x = place()
    for place_of, e in enumerate((0, 2, 1, 3)):
        zz = jnp.where(c == 0, z - f, z - e) % 4
        xx = jnp.where(c == 0, x - e, x - f) % 4
        slot = 2 * ((zz - y) % 4) + xx % 2
        top = place_of * rows
        own = xx // 2 == c

        @pl.when(own)
        def _(slot=slot, top=top):
            mine_ref[slot] = source[top : top + rows, :]

        @pl.when(jnp.logical_not(own))
        def _(slot=slot, top=top):
            theirs_ref[slot] = source[top : top + rows, :]


def arrange_body(rows, y0_ref, y1_ref, y3_ref, mine_ref, theirs_ref):
    for f, source in ((0, y0_ref), (1, y1_ref), (3, y3_ref)):
        arrange(rows, f, source, mine_ref, theirs_ref)


def output_last_body(rows, a_ref, b_ref, w_ref, mine_in, theirs_in, mine_ref, theirs_ref, y2):
    output_body(a_ref, b_ref, w_ref, y2)
    arrange(rows, 2, y2, mine_ref, theirs_ref)


def local(hidden, gain, w_query, w_key, w_value, w_out, key_cache, value_cache, lengths):
    heads = w_query.shape[1] // HD
    depth = hidden.shape[1]
    width = w_out.shape[1]
    rows = key_cache.shape[0] * NEW
    main = (heads + 2) * rows
    length = main + 16

    positions = (lengths[:, None] + jnp.arange(NEW, dtype=jnp.int32)[None, :]).reshape(-1)
    indices = jnp.arange(HD // 2, dtype=F32)
    inverse = jnp.power(F32(ROPE_BASE), -2.0 * indices / HD)
    angles = positions.astype(F32)[:, None] * inverse[None, :]
    cosine, sine = jnp.cos(angles), jnp.sin(angles)
    cosine = jnp.concatenate([cosine, cosine], 1)
    sine = jnp.concatenate([-sine, sine], 1)

    two, one, three = [shift_y(hidden, d) for d in (2, 1, 3)]
    received = [one, two, three]
    sources = [hidden, gain, w_query, w_key, w_value]
    back, own, scale, *weights = call(
        load_body,
        [pltpu.VMEM(v.shape, v.dtype) for v in [received[0]] + sources],
        [VSPEC] + [HSPEC] * 5,
        "load",
        4,
        scratch=[pltpu.SemaphoreType.DMA((6,))],
    )(received[0], *[in_hbm(v) for v in sources])
    blocks = [own, swap_core(hidden)]
    for value in [back] + received[1:]:
        blocks += [value, swap_core(value)]

    half = shape((2, length, HD))
    two_a, two_b, one_b, three_a, scaled, squares = call(
        functools.partial(project_first_body, rows, heads),
        [half] * 4 + [shape((16, rows, depth)), shape((16, 16, HD))],
        [VSPEC] * 12,
        "project_first",
        14,
    )(scale, *weights, *blocks)
    over_a, over_b = shift_first(two_a, 1), shift_first(two_b, 3)
    from_one_b, from_three_a = shift_first(one_b, 1), shift_first(three_a, 3)
    one_a, three_b, own_a, own_b = call(
        functools.partial(project_second_body, rows, heads),
        [half] * 4,
        [VSPEC] * 5,
        "project_second",
        12,
    )(scaled, squares, *weights)

    def add(terms, *values):
        return call(
            functools.partial(add_body, main, terms),
            [shape((len(picks), length, HD)) for picks in terms],
            [VSPEC] * len(values),
            "add",
            8,
        )(*values)

    pairwise = [[[(0, 0), (1, 0)], [(0, 1), (1, 1)]]]
    sum_one, sum_three = add(pairwise, one_a, over_a)[0], add(pairwise, three_b, over_b)[0]
    from_one_a, from_three_b = shift_first(sum_one, 1), shift_first(sum_three, 3)
    keys, values, token = call(
        caches_body,
        [pltpu.VMEM(v.shape, v.dtype) for v in (key_cache, value_cache)] + [shape((16, HD))],
        [VSPEC, HSPEC, HSPEC],
        "load_caches",
        4,
        scratch=[pltpu.SemaphoreType.DMA((2,))],
    )(sum_three, in_hbm(key_cache), in_hbm(value_cache))
    early, early_rest = call(
        functools.partial(
            early_sum_body,
            [[(0, 0), (3, 0)], [(0, 1), (3, 1)], [(1, 0), (2, 0)], [(1, 1), (2, 1)]],
        ),
        [shape((1, length, HD), F32), shape((3, length, HD), F32)],
        [VSPEC] * 4,
        "early_sum",
        8,
    )(own_a, own_b, from_one_b, from_three_a)
    terms = [[[(0, 1), (2, 0)]], [[(0, 0), (1, 1)]], [[(0, 2), (2, 1)]]]
    two, one, three = add(terms, early_rest, from_one_a, from_three_b, token)
    arrived = [shift_second(two, 2), shift_second(one, 1), shift_second(three, 3)]
    parts = [early, from_one_a] + arrived

    context, fresh_keys, fresh_values = call(
        functools.partial(attend_body, rows, heads),
        [shape((rows, heads * HD)), shape((rows, HD)), shape((rows, HD))],
        [SSPEC] + [VSPEC] * 9,
        "attend",
        10,
        scratch=[
            pltpu.VMEM((rows * heads, HD), F32),
            pltpu.VMEM((rows * heads, HD), F32),
            pltpu.VMEM((rows, HD), F32),
            pltpu.VMEM((rows, HD), F32),
        ],
    )(lengths, *parts, cosine, sine, keys, values)

    context = call(
        together_body,
        [shape(context.shape)],
        [VSPEC] * 2,
        "together",
        4,
    )(swap_core(fresh_keys), context)[0]
    two, one, three = [shift_first(context, e) for e in (2, 1, 3)]
    low, high = jnp.concatenate([context, two], 0), jnp.concatenate([one, three], 0)
    one_low, three_high = shift_second(low, 1), shift_second(high, 3)
    two_low, two_high = shift_second(one_low, 1), shift_second(three_high, 3)
    one_high, three_low = shift_second(high, 1), shift_second(low, 3)

    def project_out(a, b):
        return call(
            output_body,
            [shape((4 * rows, width))],
            [VSPEC] * 3,
            "project_out",
            8,
        )(a, b, w_out)[0]

    arranged = [shape((8, rows, width)), shape((8, rows, width))]
    near = call(functools.partial(arrange_body, rows), arranged, [VSPEC] * 3, "arrange", 8)(
        project_out(low, high),
        project_out(one_low, one_high),
        project_out(three_low, three_high),
    )
    mine, theirs = call(
        functools.partial(output_last_body, rows),
        arranged,
        [VSPEC] * 5,
        "project_out_last",
        12,
        scratch=[pltpu.VMEM((4 * rows, width), BF16)],
        aliases={3: 0, 4: 1},
    )(two_low, two_high, w_out, *near)
    both = mine.astype(F32) + swap_core(theirs).astype(F32)
    over_a, over_b = shift_y(both[4].astype(BF16), 1), shift_y(both[5].astype(BF16), 3)
    from_one_b, from_three_a = shift_y(both[3].astype(BF16), 1), shift_y(both[6].astype(BF16), 3)
    from_one_a = shift_y((both[2] + over_a.astype(F32)).astype(BF16), 1)
    from_three_b = shift_y((both[7] + over_b.astype(F32)).astype(BF16), 3)
    upper = both[0] + from_one_a.astype(F32) + from_three_a.astype(F32)
    lower = both[1] + from_one_b.astype(F32) + from_three_b.astype(F32)
    result = hidden.astype(F32) + jnp.concatenate([upper, lower], axis=0)
    return result.astype(BF16), fresh_keys, fresh_values


def solution(mesh):
    return jax.shard_map(
        local,
        mesh=mesh,
        in_specs=(
            P("gx", "gy"),
            P("gy"),
            P("gy", "gx"),
            P("gy", "gx"),
            P("gy", "gx"),
            P("gx", "gy"),
            P("gy", None, "gx"),
            P("gy", None, "gx"),
            P("gy"),
        ),
        out_specs=(P("gx", "gy"), P("gy", "gx"), P("gy", "gx")),
        check_vma=False,
    )
```

```python
import functools

import jax
import jax.numpy as jnp
from jax import lax
from jax.experimental import pallas as pl
from jax.experimental.pallas import tpu as pltpu
from jax.sharding import PartitionSpec as P

D = 16384
HD = 128
NEW = 2
EPSILON = 1e-05
ROPE_BASE = 500000.0

NY = NZ = NX = 4
NC = 2
AXES = ("gx", "gy")
BF16 = jnp.bfloat16
F32 = jnp.float32
MIB = 1024 * 1024
TOGETHER = 8
STEP = 64
LOG2_E = 1.4426950408889634


def pairs(move):
    out = []
    for y in range(NY):
        for c in range(NC):
            for z in range(NZ):
                for x in range(NX):
                    y2, c2, z2, x2 = move(y, c, z, x)
                    source = ((y * NC + c) * NZ + z) * NX + x
                    target = (((y2 % NY) * NC + c2 % NC) * NZ + z2 % NZ) * NX + x2 % NX
                    out.append((source, target))
    return out


def swap_core(value):
    return lax.ppermute(value, AXES, pairs(lambda y, c, z, x: (y, c + 1, z, x)))


def shift_y(value, step):
    return lax.ppermute(value, AXES, pairs(lambda y, c, z, x: (y + step, c, z, x)))


def shift_first(value, step):
    def move(y, c, z, x):
        return (y, c, z, x + step) if c == 0 else (y, c, z + step, x)

    return lax.ppermute(value, AXES, pairs(move))


def shift_second(value, step):
    def move(y, c, z, x):
        return (y, c, z + step, x) if c == 0 else (y, c, z, x + step)

    return lax.ppermute(value, AXES, pairs(move))


VSPEC = pl.BlockSpec(memory_space=pltpu.VMEM)
SSPEC = pl.BlockSpec(memory_space=pltpu.SMEM)
HSPEC = pl.BlockSpec(memory_space=pltpu.HBM)


def call(body, outs, in_specs, name, vmem, scratch=(), aliases={}):
    return pl.pallas_call(
        body,
        out_shape=outs,
        in_specs=in_specs,
        out_specs=[VSPEC] * len(outs),
        scratch_shapes=list(scratch),
        compiler_params=pltpu.CompilerParams(vmem_limit_bytes=vmem * MIB),
        cost_estimate=pl.CostEstimate(flops=0, bytes_accessed=0, transcendentals=0),
        input_output_aliases=aliases,
        name=name,
    )


def shape(dims, dtype=BF16):
    return jax.ShapeDtypeStruct(dims, dtype)


def in_hbm(value):
    return pltpu.with_memory_space_constraint(value, pltpu.HBM)


def place():
    gx, gy = lax.axis_index("gx"), lax.axis_index("gy")
    return gx // NC, gx % NC, gy // NX, gy % NX


def split_high_low(total):
    high = total.astype(BF16).astype(F32)
    return jnp.concatenate([high, total - high], axis=0).astype(BF16)


def load_body(back_ref, hidden_hbm, gain_hbm, wq_hbm, wk_hbm, wv_hbm, *refs):
    outs, sems = refs[:-1], refs[-1]
    sources = (back_ref, hidden_hbm, gain_hbm, wq_hbm, wk_hbm, wv_hbm)
    copies = [
        pltpu.make_async_copy(source, out, sems.at[i])
        for i, (source, out) in enumerate(zip(sources, outs))
    ]
    for copy in copies:
        copy.start()
    for copy in copies:
        copy.wait()


def project_blocks(rows, heads, first, hs, sq, wq_ref, wk_ref, wv_ref, outs):
    per = outs[0].shape[0]
    count = per * len(outs)
    lhs = hs[first : first + count].reshape(count * rows, hs.shape[2])
    for n in range(heads // 2 + 1):
        if n == heads // 2:
            rhs = jnp.concatenate([wk_ref[...], wv_ref[...]], axis=1)
        else:
            rhs = wq_ref[:, n * 256 : (n + 1) * 256]
        acc = jnp.dot(lhs, rhs, preferred_element_type=F32).astype(BF16)
        for i in range(count):
            for hh in range(2):
                head = 2 * n + hh
                outs[i // per][i % per, head * rows : (head + 1) * rows, :] = acc[
                    i * rows : (i + 1) * rows, hh * HD : (hh + 1) * HD
                ]
    for i in range(count):
        outs[i // per][i % per, (heads + 2) * rows :, :] = sq[first + i]


def project_first_body(rows, heads, gain_ref, wq_ref, wk_ref, wv_ref, *refs):
    blocks, outs, (hs, sq) = refs[:8], refs[8:12], refs[12:]
    y, c, z, x = place()
    gain = gain_ref[...].astype(F32).reshape(1, -1)
    depth = gain.shape[1]
    pad = jnp.zeros((HD - rows, HD), F32)
    for i, block in enumerate(blocks):
        for j in range(2):
            dz = (y - i // 2 - z) % 4
            dx = (2 * (c ^ (i % 2)) + j - x) % 4
            e, f = jnp.where(c == 0, dx, dz), jnp.where(c == 0, dz, dx)
            slot = jnp.where(e == 2, f, 12 + f)
            slot = jnp.where(e == 1, jnp.where(f >= 2, 2 + f, 8 + f), slot)
            slot = jnp.where(e == 3, jnp.where(f < 2, 6 + f, 8 + f), slot)
            parts = []
            for top in range(0, rows, 16):
                value = block[j * rows + top : j * rows + top + 16, :].astype(F32)
                hs[slot, top : top + 16, :] = (value * gain).astype(BF16)
                parts.append(
                    sum(value[:, n : n + HD] * value[:, n : n + HD] for n in range(0, depth, HD))
                )
            turned = jnp.transpose(jnp.concatenate(parts + [pad], axis=0))
            total = jnp.broadcast_to(jnp.sum(turned, axis=0, keepdims=True), (8, HD))
            sq[slot] = split_high_low(total)
    project_blocks(rows, heads, 0, hs, sq, wq_ref, wk_ref, wv_ref, outs)


def project_second_body(rows, heads, hs, sq, wq_ref, wk_ref, wv_ref, *outs):
    project_blocks(rows, heads, 8, hs, sq, wq_ref, wk_ref, wv_ref, outs)


def caches_body(after_ref, kc_hbm, vc_hbm, kc_ref, vc_ref, token_ref, sems):
    copies = [
        pltpu.make_async_copy(kc_hbm, kc_ref, sems.at[0]),
        pltpu.make_async_copy(vc_hbm, vc_ref, sems.at[1]),
    ]
    for copy in copies:
        copy.start()
    token_ref[...] = jnp.zeros_like(token_ref)
    for copy in copies:
        copy.wait()


def add_body(main, terms, *refs):
    ins, outs = refs[: len(refs) - len(terms)], refs[len(refs) - len(terms) :]
    for out, picks in zip(outs, terms):
        for i, pick in enumerate(picks):
            for top in range(0, main, STEP):
                total = sum(ins[ref][block, top : top + STEP, :].astype(F32) for ref, block in pick)
                out[i, top : top + STEP, :] = total.astype(BF16)
            total = sum(ins[ref][block, main:, :].astype(F32) for ref, block in pick)
            out[i, main:, :] = split_high_low(total[:8] + total[8:])


def early_sum_body(picks, *refs):
    ins, outs = refs[:4], refs[4:]
    for (out, at), pick in zip(((outs[0], 0), (outs[1], 0), (outs[1], 1), (outs[1], 2)), picks):
        out[at] = sum(ins[ref][block].astype(F32) for ref, block in pick)


def attend_body(
    rows, heads, len_ref, p0_ref, p1_ref, r1_ref, r2_ref, r3_ref,
    cos_ref, sin_ref, kbuf, vbuf,
    ctx_ref, nk_ref, nv_ref, qs, os, kf, vf,
):
    seqs = rows // NEW
    slots = kbuf.shape[1]
    main = (heads + 2) * rows

    def total(lo, hi):
        refs = (p0_ref, p1_ref, r1_ref, r2_ref, r3_ref)
        return sum(ref[0, lo:hi, :].astype(F32) for ref in refs)

    square = total(main, main + 16)
    column = jnp.transpose(square[:8] + square[8:])[:rows, 0:1]
    scales = lax.rsqrt(column / D + EPSILON)
    cosine, sine = cos_ref[...], sin_ref[...]

    def rope(value):
        return value * cosine + pltpu.roll(value, HD // 2, 1) * sine

    for head in range(heads):
        value = total(head * rows, (head + 1) * rows) * scales
        qs[pl.ds(head, rows, stride=heads), :] = rope(value).astype(BF16).astype(F32)
    key = rope(total(heads * rows, (heads + 1) * rows) * scales).astype(BF16)
    nk_ref[...] = key
    kf[...] = key.astype(F32)
    fresh = (total((heads + 1) * rows, (heads + 2) * rows) * scales).astype(BF16)
    nv_ref[...] = fresh
    vf[...] = fresh.astype(F32)

    per = NEW * heads
    scale = HD ** (-0.5) * LOG2_E
    slot_of = lax.broadcasted_iota(jnp.int32, (1, slots), 1)
    second = lax.broadcasted_iota(jnp.int32, (per, 1), 0) >= heads

    def several(first, count):
        ids = [first + u for u in range(count)]
        query = [qs[pl.ds(pl.multiple_of(s * per, per), per), :] for s in ids]
        scores = [
            lax.dot_general(
                q.astype(BF16), kbuf[s], (((1,), (1,)), ((), ())), preferred_element_type=F32
            )
            for q, s in zip(query, ids)
        ]
        scores = [
            v + jnp.where(slot_of < len_ref[s], 0.0, -jnp.inf) for v, s in zip(scores, ids)
        ]
        s0 = [jnp.sum(q * kf[pl.ds(2 * s, 1), :], axis=1, keepdims=True) for q, s in zip(query, ids)]
        s1 = [
            jnp.where(
                second,
                jnp.sum(q * kf[pl.ds(2 * s + 1, 1), :], axis=1, keepdims=True),
                -jnp.inf,
            )
            for q, s in zip(query, ids)
        ]
        highest = [
            jnp.maximum(jnp.max(v, axis=1, keepdims=True), jnp.maximum(a, b))
            for v, a, b in zip(scores, s0, s1)
        ]
        probs = [jnp.exp2((v - m) * scale) for v, m in zip(scores, highest)]
        p0 = [jnp.exp2((v - m) * scale) for v, m in zip(s0, highest)]
        p1 = [jnp.exp2((v - m) * scale) for v, m in zip(s1, highest)]
        norm = [
            1.0 / (jnp.sum(v, axis=1, keepdims=True) + a + b) for v, a, b in zip(probs, p0, p1)
        ]
        out = [
            jnp.dot(v.astype(BF16), vbuf[s], preferred_element_type=F32)
            for v, s in zip(probs, ids)
        ]
        for u, s in enumerate(ids):
            w0, w1 = p0[u].astype(BF16).astype(F32), p1[u].astype(BF16).astype(F32)
            os[pl.ds(pl.multiple_of(s * per, per), per), :] = (
                out[u] + w0 * vf[pl.ds(2 * s, 1), :] + w1 * vf[pl.ds(2 * s + 1, 1), :]
            ) * norm[u]

    def step(i, carry):
        several(TOGETHER * i, TOGETHER)
        return carry

    lax.fori_loop(0, seqs // TOGETHER, step, 0)
    for head in range(heads):
        ctx_ref[:, head * HD : (head + 1) * HD] = os[pl.ds(head, rows, stride=heads), :].astype(BF16)


def together_body(token_ref, a_ref, out_ref):
    out_ref[...] = a_ref[...]


def output_body(a_ref, b_ref, w_ref, out_ref):
    lhs = jnp.concatenate([a_ref[...], b_ref[...]], axis=0)
    for n in range(w_ref.shape[1] // 256):
        cols = slice(n * 256, (n + 1) * 256)
        out_ref[:, cols] = jnp.dot(lhs, w_ref[:, cols], preferred_element_type=F32).astype(BF16)


def arrange(rows, f, source, mine_ref, theirs_ref):
    y, c, z, x = place()
    for place_of, e in enumerate((0, 2, 1, 3)):
        zz = jnp.where(c == 0, z - f, z - e) % 4
        xx = jnp.where(c == 0, x - e, x - f) % 4
        slot = 2 * ((zz - y) % 4) + xx % 2
        top = place_of * rows
        own = xx // 2 == c

        @pl.when(own)
        def _(slot=slot, top=top):
            mine_ref[slot] = source[top : top + rows, :]

        @pl.when(jnp.logical_not(own))
        def _(slot=slot, top=top):
            theirs_ref[slot] = source[top : top + rows, :]


def arrange_body(rows, y0_ref, y1_ref, y3_ref, mine_ref, theirs_ref):
    for f, source in ((0, y0_ref), (1, y1_ref), (3, y3_ref)):
        arrange(rows, f, source, mine_ref, theirs_ref)


def output_last_body(rows, a_ref, b_ref, w_ref, mine_in, theirs_in, mine_ref, theirs_ref, y2):
    output_body(a_ref, b_ref, w_ref, y2)
    arrange(rows, 2, y2, mine_ref, theirs_ref)


def base_body(hidden_ref, mine_ref, swapped_ref, upper_ref, lower_ref, out_ref):
    rows = upper_ref.shape[0]
    for j, sent in enumerate((upper_ref, lower_ref)):
        part = slice(j * rows, (j + 1) * rows)
        total = mine_ref[j].astype(F32) + swapped_ref[j].astype(F32) + sent[...].astype(F32)
        out_ref[part, :] = hidden_ref[part, :].astype(F32) + total


def local(hidden, gain, w_query, w_key, w_value, w_out, key_cache, value_cache, lengths):
    heads = w_query.shape[1] // HD
    depth = hidden.shape[1]
    width = w_out.shape[1]
    rows = key_cache.shape[0] * NEW
    main = (heads + 2) * rows
    length = main + 16

    positions = (lengths[:, None] + jnp.arange(NEW, dtype=jnp.int32)[None, :]).reshape(-1)
    indices = jnp.arange(HD // 2, dtype=F32)
    inverse = jnp.power(F32(ROPE_BASE), -2.0 * indices / HD)
    angles = positions.astype(F32)[:, None] * inverse[None, :]
    cosine, sine = jnp.cos(angles), jnp.sin(angles)
    cosine = jnp.concatenate([cosine, cosine], 1)
    sine = jnp.concatenate([-sine, sine], 1)

    two, one, three = [shift_y(hidden, d) for d in (2, 1, 3)]
    received = [one, two, three]
    sources = [hidden, gain, w_query, w_key, w_value]
    back, own, scale, *weights = call(
        load_body,
        [pltpu.VMEM(v.shape, v.dtype) for v in [received[0]] + sources],
        [VSPEC] + [HSPEC] * 5,
        "load",
        4,
        scratch=[pltpu.SemaphoreType.DMA((6,))],
    )(received[0], *[in_hbm(v) for v in sources])
    blocks = [own, swap_core(hidden)]
    for value in [back] + received[1:]:
        blocks += [value, swap_core(value)]

    half = shape((2, length, HD))
    two_a, two_b, one_b, three_a, scaled, squares = call(
        functools.partial(project_first_body, rows, heads),
        [half] * 4 + [shape((16, rows, depth)), shape((16, 16, HD))],
        [VSPEC] * 12,
        "project_first",
        14,
    )(scale, *weights, *blocks)
    over_a, over_b = shift_first(two_a, 1), shift_first(two_b, 3)
    from_one_b, from_three_a = shift_first(one_b, 1), shift_first(three_a, 3)
    one_a, three_b, own_a, own_b = call(
        functools.partial(project_second_body, rows, heads),
        [half] * 4,
        [VSPEC] * 5,
        "project_second",
        12,
    )(scaled, squares, *weights)

    def add(terms, *values):
        return call(
            functools.partial(add_body, main, terms),
            [shape((len(picks), length, HD)) for picks in terms],
            [VSPEC] * len(values),
            "add",
            8,
        )(*values)

    pairwise = [[[(0, 0), (1, 0)], [(0, 1), (1, 1)]]]
    sum_one, sum_three = add(pairwise, one_a, over_a)[0], add(pairwise, three_b, over_b)[0]
    from_one_a, from_three_b = shift_first(sum_one, 1), shift_first(sum_three, 3)
    keys, values, token = call(
        caches_body,
        [pltpu.VMEM(v.shape, v.dtype) for v in (key_cache, value_cache)] + [shape((16, HD))],
        [VSPEC, HSPEC, HSPEC],
        "load_caches",
        4,
        scratch=[pltpu.SemaphoreType.DMA((2,))],
    )(sum_three, in_hbm(key_cache), in_hbm(value_cache))
    early, early_rest = call(
        functools.partial(
            early_sum_body,
            [[(0, 0), (3, 0)], [(0, 1), (3, 1)], [(1, 0), (2, 0)], [(1, 1), (2, 1)]],
        ),
        [shape((1, length, HD), F32), shape((3, length, HD), F32)],
        [VSPEC] * 4,
        "early_sum",
        8,
    )(own_a, own_b, from_one_b, from_three_a)
    terms = [[[(0, 1), (2, 0)]], [[(0, 0), (1, 1)]], [[(0, 2), (2, 1)]]]
    two, one, three = add(terms, early_rest, from_one_a, from_three_b, token)
    arrived = [shift_second(two, 2), shift_second(one, 1), shift_second(three, 3)]
    parts = [early, from_one_a] + arrived

    context, fresh_keys, fresh_values = call(
        functools.partial(attend_body, rows, heads),
        [shape((rows, heads * HD)), shape((rows, HD)), shape((rows, HD))],
        [SSPEC] + [VSPEC] * 9,
        "attend",
        10,
        scratch=[
            pltpu.VMEM((rows * heads, HD), F32),
            pltpu.VMEM((rows * heads, HD), F32),
            pltpu.VMEM((rows, HD), F32),
            pltpu.VMEM((rows, HD), F32),
        ],
    )(lengths, *parts, cosine, sine, keys, values)

    context = call(
        together_body,
        [shape(context.shape)],
        [VSPEC] * 2,
        "together",
        4,
    )(swap_core(fresh_keys), context)[0]
    two, one, three = [shift_first(context, e) for e in (2, 1, 3)]
    low, high = jnp.concatenate([context, two], 0), jnp.concatenate([one, three], 0)
    one_low, three_high = shift_second(low, 1), shift_second(high, 3)
    two_low, two_high = shift_second(one_low, 1), shift_second(three_high, 3)
    one_high, three_low = shift_second(high, 1), shift_second(low, 3)

    def project_out(a, b):
        return call(
            output_body,
            [shape((4 * rows, width))],
            [VSPEC] * 3,
            "project_out",
            8,
        )(a, b, w_out)[0]

    arranged = [shape((8, rows, width)), shape((8, rows, width))]
    near = call(functools.partial(arrange_body, rows), arranged, [VSPEC] * 3, "arrange", 8)(
        project_out(low, high),
        project_out(one_low, one_high),
        project_out(three_low, three_high),
    )
    mine, theirs = call(
        functools.partial(output_last_body, rows),
        arranged,
        [VSPEC] * 5,
        "project_out_last",
        12,
        scratch=[pltpu.VMEM((4 * rows, width), BF16)],
        aliases={3: 0, 4: 1},
    )(two_low, two_high, w_out, *near)
    swapped = swap_core(theirs)
    both = mine.astype(F32) + swapped.astype(F32)
    over_a, over_b = shift_y(both[4].astype(BF16), 1), shift_y(both[5].astype(BF16), 3)
    from_one_b, from_three_a = shift_y(both[3].astype(BF16), 1), shift_y(both[6].astype(BF16), 3)
    from_one_a = shift_y((both[2] + over_a.astype(F32)).astype(BF16), 1)
    from_three_b = shift_y((both[7] + over_b.astype(F32)).astype(BF16), 3)
    base = call(
        base_body,
        [shape(hidden.shape, F32)],
        [VSPEC] * 5,
        "base",
        8,
    )(hidden, mine, swapped, from_three_a, from_one_b)[0]
    result = base + jnp.concatenate([from_one_a, from_three_b], axis=0).astype(F32)
    return result.astype(BF16), fresh_keys, fresh_values


def solution(mesh):
    return jax.shard_map(
        local,
        mesh=mesh,
        in_specs=(
            P("gx", "gy"),
            P("gy"),
            P("gy", "gx"),
            P("gy", "gx"),
            P("gy", "gx"),
            P("gx", "gy"),
            P("gy", None, "gx"),
            P("gy", None, "gx"),
            P("gy"),
        ),
        out_specs=(P("gx", "gy"), P("gy", "gx"), P("gy", "gx")),
        check_vma=False,
    )
```
